32 devices in a mesh: coil: 2 (over x), ro: 16 (over z, y, core).
Axes of the slice: x: 2, y: 2, z: 4, core: 2. Of those that a mesh axis runs over, the one named last changes fastest.
Arguments:
- kspace: bfloat16 [2, 64, 16, 448, 320], P(None, 'coil', None, 'ro'), may hold values from -884272563206990856199 to 884272563206990856199
- sensitivity: bfloat16 [2, 64, 16, 448, 320], P(None, 'coil', 'ro'), may hold values from -0.75 to 0.75
- sampled: int32 [16, 448], replicated, may hold values 0 or 1
- pole_y: int32 [16, 320], replicated, may hold values from 4 to 112
- order_y: int32 [16, 320], replicated, may hold values from 1 to 3
- pole_z: int32 [16, 448], replicated, may hold values from 4 to 80
- order_z: int32 [16, 448], replicated, may hold values from 1 to 3
Outputs:
- image: float32 [2, 16, 448, 320], P(None, 'ro', 'coil')
The draws below stay inside these ranges and needn't reach their ends.
All inputs are finite; a program needn't handle non-finite values.
Results may differ from the reference program's by a relative error of at most 0.0056.
Values may be sent and summed in bfloat16 or wider, within the bound.
No kernel may reach another device: no remote copies, remote signals or barrier semaphores. Data moves between devices by JAX's collectives and lax.ppermute only.
A program may use at most 192 MiB of HBM per device.

```python
import math
import jax
import jax.numpy as jnp
from jax import lax

C = 64
KY = 448
KZ = 320
RO = 16


def window_params(key):
    pole_rows = jax.random.randint(jax.random.fold_in(key, 101), (RO, KZ), 4, KY // 4 + 1, dtype=jnp.int32)
    order_rows = jax.random.randint(jax.random.fold_in(key, 102), (RO, KZ), 1, 4, dtype=jnp.int32)
    pole_cols = jax.random.randint(jax.random.fold_in(key, 103), (RO, KY), 4, KZ // 4 + 1, dtype=jnp.int32)
    order_cols = jax.random.randint(jax.random.fold_in(key, 104), (RO, KY), 1, 4, dtype=jnp.int32)
    return (pole_rows, order_rows, pole_cols, order_cols)


def draw_pole_y(key, part):
    return window_params(key)[0]


def draw_order_y(key, part):
    return window_params(key)[1]


def draw_pole_z(key, part):
    return window_params(key)[2]


def draw_order_z(key, part):
    return window_params(key)[3]


def draw_kspace(key, part):
    pole_rows, order_rows, pole_cols, order_cols = window_params(key)
    index_y = jnp.arange(KY, dtype=jnp.int32)
    freq_y = jnp.minimum(index_y, KY - index_y).astype(jnp.float32)
    index_z = jnp.arange(KZ, dtype=jnp.int32)
    freq_z = jnp.minimum(index_z, KZ - index_z).astype(jnp.float32)
    ratio_y = freq_y[None, :, None] / pole_rows[:, None, :].astype(jnp.float32)
    growth_y = 1.0 + jnp.power(ratio_y, 2.0 * order_rows[:, None, :].astype(jnp.float32))
    ratio_z = freq_z[None, None, :] / pole_cols[:, :, None].astype(jnp.float32)
    growth_z = 1.0 + jnp.power(ratio_z, 2.0 * order_cols[:, :, None].astype(jnp.float32))
    noise_key = jax.random.fold_in(key, 111)
    values = jnp.clip(jax.random.normal(noise_key, (2, C, RO, KY, KZ), jnp.float32), -6.0, 6.0)
    return (values * (growth_y * growth_z)[None, None]).astype(jnp.bfloat16)


def with_ends(array, key, smallest, top_value):
    dims = array.shape
    place = [jax.random.randint(jax.random.fold_in(key, axis), (), 0, dims[axis]) for axis in range(len(dims))]
    array = array.at[tuple(place)].set(smallest)
    longest = dims.index(max(dims))
    place[longest] = (place[longest] + 1) % dims[longest]
    return array.at[tuple(place)].set(top_value)


def raised(entries, own_key, source, target, shards_of, factor):
    owner, partner = [(jnp.arange(entries.shape[position]) // (entries.shape[position] // shards_of)).reshape([-1 if axis == position else 1 for axis in range(entries.ndim)]) for position in (source, target)]
    chosen = jax.random.permutation(own_key, shards_of)[partner]
    strong = (owner == chosen) | (owner == (partner + shards_of // 2) % shards_of)
    return jnp.where(strong, factor * entries, entries)


def levels(own_key, extent, cuts, least, top_value):
    loudness = 1.0
    for axis_at, blocks in cuts:
        draws = jax.random.uniform(jax.random.fold_in(jax.random.fold_in(own_key, 6), axis_at), (blocks,), jnp.float32, least / len(cuts), top_value / len(cuts))
        loudness = loudness * jnp.repeat(jnp.exp(draws), extent[axis_at] // blocks).reshape((-1,) + (1,) * (len(extent) - 1 - axis_at))
    return loudness


def noise_with(key, shape, spread, reach, shards, heavy, kind=jnp.bfloat16):
    result = spread * jax.random.normal(key, shape, jnp.float32)
    if shards:
        result = result * levels(key, shape, shards, -0.22, 0.18)
    return jnp.clip(raised(result, jax.random.fold_in(key, 3), *heavy), -reach, reach).astype(kind)


def setup_inputs(seed: int = 0) -> dict:
    key_list = jax.random.split(jax.random.key(seed), 8)
    return {
        "kspace": draw_kspace(jax.random.fold_in(key_list[7], 71), 0),
        "sensitivity": noise_with(key_list[1], (2, C, RO, KY, KZ), (2 * C) ** -0.5, 0.75, ((1, 2), (2, 16)), (1, 3, 2, 2.0)),
        "sampled": with_ends((jax.random.randint(key_list[2], (RO, KY), 0, 4) < 3).astype(jnp.int32), jax.random.fold_in(key_list[2], 1), 0, 1),
        "pole_y": draw_pole_y(jax.random.fold_in(key_list[7], 71), 0),
        "order_y": draw_order_y(jax.random.fold_in(key_list[7], 71), 0),
        "pole_z": draw_pole_z(jax.random.fold_in(key_list[7], 71), 0),
        "order_z": draw_order_z(jax.random.fold_in(key_list[7], 71), 0),
    }


def dft_tables(length):
    index = jnp.arange(length, dtype=jnp.int32)
    product = index[:, None] * index[None, :] % length
    angle = product.astype(jnp.float32) * (2.0 * math.pi / length)
    factor = 1.0 / math.sqrt(length)
    return ((jnp.cos(angle) * factor).astype(jnp.bfloat16), (jnp.sin(angle) * factor).astype(jnp.bfloat16))

def line_window(frequency, pole, degree):
    quotient = frequency / pole.astype(jnp.float32)
    return 1.0 / (1.0 + jnp.power(quotient, 2.0 * degree.astype(jnp.float32)))

def fold_freq(length):
    index = jnp.arange(length, dtype=jnp.int32)
    return jnp.minimum(index, length - index).astype(jnp.float32)

def reference(kspace, sensitivity, sampled, pole_y, order_y, pole_z, order_z):
    kz_cosine, kz_sine = dft_tables(KZ)
    ky_cosine, ky_sine = dft_tables(KY)
    freq_y = fold_freq(KY)
    freq_z = fold_freq(KZ)
    high = lax.Precision.HIGHEST

    def recon_one(readout):
        block = lax.dynamic_index_in_dim(kspace, readout, 2, keepdims=False)
        maps = lax.dynamic_index_in_dim(sensitivity, readout, 2, keepdims=False).astype(jnp.float32)
        weight_y = sampled[readout][:, None].astype(jnp.float32) * line_window(freq_y[:, None], pole_y[readout][None, :], order_y[readout][None, :])
        weight_z = line_window(freq_z[None, :], pole_z[readout][:, None], order_z[readout][:, None])
        filtered = (block.astype(jnp.float32) * weight_y * weight_z).astype(jnp.bfloat16).astype(jnp.float32)
        real_part, imag_part = (filtered[0], filtered[1])
        cos_z = kz_cosine.astype(jnp.float32)
        sin_z = kz_sine.astype(jnp.float32)
        hyb_real = jnp.einsum('ckz,zn->ckn', real_part, cos_z, precision=high) - jnp.einsum('ckz,zn->ckn', imag_part, sin_z, precision=high)
        hyb_imag = jnp.einsum('ckz,zn->ckn', real_part, sin_z, precision=high) + jnp.einsum('ckz,zn->ckn', imag_part, cos_z, precision=high)
        hyb_real = hyb_real.astype(jnp.bfloat16).astype(jnp.float32)
        hyb_imag = hyb_imag.astype(jnp.bfloat16).astype(jnp.float32)
        cos_y = ky_cosine.astype(jnp.float32)
        sin_y = ky_sine.astype(jnp.float32)
        img_real = jnp.einsum('nk,ckz->cnz', cos_y, hyb_real, precision=high) - jnp.einsum('nk,ckz->cnz', sin_y, hyb_imag, precision=high)
        img_imag = jnp.einsum('nk,ckz->cnz', sin_y, hyb_real, precision=high) + jnp.einsum('nk,ckz->cnz', cos_y, hyb_imag, precision=high)
        out_real = lax.optimization_barrier(jnp.sum(maps[0] * img_real + maps[1] * img_imag, axis=0))
        out_imag = lax.optimization_barrier(jnp.sum(maps[0] * img_imag - maps[1] * img_real, axis=0))
        return jnp.stack([out_real, out_imag])
    stacked = lax.map(recon_one, jnp.arange(RO, dtype=jnp.int32))
    return jnp.transpose(stacked, (1, 0, 2, 3))
```

```python
import functools
import math

import jax
import jax.numpy as jnp
import ml_dtypes
import numpy as np
from jax import lax
from jax.experimental import pallas as pl
from jax.experimental.pallas import tpu as pltpu
from jax.sharding import PartitionSpec as P

LANES = 128
VMEM_BYTES = 56 * 2**20
PLAN = (3, 4, 1)


def round_up(value, step):
    return (value + step - 1) // step * step


def dft_tables(length):
    index = np.arange(length, dtype=np.int64)
    product = index[:, None] * index[None, :] % length
    angle = product.astype(np.float32) * np.float32(2.0 * math.pi / length)
    factor = np.float32(1.0 / math.sqrt(length))
    return (
        (np.cos(angle) * factor).astype(ml_dtypes.bfloat16).astype(np.float32),
        (np.sin(angle) * factor).astype(ml_dtypes.bfloat16).astype(np.float32),
    )


def kz_table(length, half):
    cosine, sine = dft_tables(length)
    table = np.zeros((2 * length, 2 * half), np.float32)
    table[:length, :length] = cosine
    table[length:, :length] = -sine
    table[:length, half : half + length] = sine
    table[length:, half : half + length] = cosine
    return jnp.asarray(table.astype(ml_dtypes.bfloat16))


def ky_table(length, groups, stride):
    lines = length // groups
    parts = []
    for part in dft_tables(length):
        padded = np.zeros((length, groups, stride), np.float32)
        padded[:, :, :lines] = part.reshape(length, groups, lines)
        parts.append(padded.reshape(length, groups * stride))
    return jnp.asarray(np.concatenate(parts, axis=1).astype(ml_dtypes.bfloat16))


def growth(frequency, pole, order):
    quotient = frequency / pole
    square = quotient * quotient
    fourth = square * square
    return 1.0 + jnp.where(order < 1.5, square, jnp.where(order < 2.5, fourth, fourth * square))


def fold(index, length):
    return jnp.minimum(index, length - index).astype(jnp.float32)


def filter_kernel(
    readouts, group, lines, first_ref, x_ref, sampled_ref, pole_y_ref, order_y_ref, pole_z_ref, order_z_ref, o_ref, weight, packed
):
    kz_count = x_ref.shape[-1]
    ky_count = sampled_ref.shape[-1]

    @pl.when(pl.program_id(0) == 0)
    def _():
        first = first_ref[0]
        rows = round_up(lines, 8)
        line = lax.broadcasted_iota(jnp.int32, (rows, ky_count), 0) + first
        place = lax.broadcasted_iota(jnp.int32, (rows, ky_count), 1)
        pick = (line == place).astype(jnp.bfloat16)

        def mine(ref):
            return lax.dot_general(
                pick,
                ref[...].astype(jnp.float32).astype(jnp.bfloat16),
                (((1,), (1,)), ((), ())),
                preferred_element_type=jnp.float32,
            )

        sampled, pole_z, order_z = mine(sampled_ref), mine(pole_z_ref), mine(order_z_ref)
        freq_y = fold(lax.broadcasted_iota(jnp.int32, (rows, kz_count), 0) + first, ky_count)
        freq_z = fold(lax.broadcasted_iota(jnp.int32, (rows, kz_count), 1), kz_count)
        for r in range(readouts):
            column_y = growth(
                freq_y, pole_y_ref[r : r + 1, :].astype(jnp.float32), order_y_ref[r : r + 1, :].astype(jnp.float32)
            )
            column_z = growth(freq_z, pole_z[:, r : r + 1], order_z[:, r : r + 1])
            weight[r] = (sampled[:, r : r + 1] / (column_y * column_z))[:lines]

    def one(r, _):
        w = weight[r]
        for c in range(group):
            for part in range(2):
                packed[pl.ds(lines * c, lines), pl.ds(part * kz_count, kz_count)] = (
                    x_ref[part, c, r].astype(jnp.float32) * w
                )
        o_ref[r] = packed[...].astype(jnp.bfloat16)
        return 0

    lax.fori_loop(0, readouts, one, 0)


def filter_chunk(kspace, first_line, params, group, first_unit, units):
    _, _, readouts, lines, kz_count = kspace.shape
    rows = group * lines
    whole = [pl.BlockSpec(p.shape, lambda i, first: (0, 0)) for p in params]
    return pl.pallas_call(
        functools.partial(filter_kernel, readouts, group, lines),
        out_shape=jax.ShapeDtypeStruct((readouts, units * rows, 2 * kz_count), jnp.bfloat16),
        grid_spec=pltpu.PrefetchScalarGridSpec(
            num_scalar_prefetch=1,
            grid=(units,),
            in_specs=[
                pl.BlockSpec((2, group, readouts, lines, kz_count), lambda i, first: (0, i + first_unit, 0, 0, 0)),
                *whole,
            ],
            out_specs=pl.BlockSpec((readouts, rows, 2 * kz_count), lambda i, first: (0, i, 0)),
            scratch_shapes=[
                pltpu.VMEM((readouts, lines, kz_count), jnp.float32),
                pltpu.VMEM((rows, 2 * kz_count), jnp.float32),
            ],
        ),
        compiler_params=pltpu.CompilerParams(vmem_limit_bytes=VMEM_BYTES),
        cost_estimate=pl.CostEstimate(
            flops=0, bytes_accessed=5 * units * readouts * rows * 2 * kz_count, transcendentals=0
        ),
        name="window_lines",
    )(first_line, kspace, *params)


def image_kernel(group, lines, stride, fresh, last, halves, me_ref, x_ref, maps_ref, kz_ref, ky_ref, *refs):
    refs = list(refs)
    acc_in = None if fresh else refs.pop(0)
    outs, (wide, hybrid, acc) = refs[:-3], refs[-3:]
    sources, rows, packed = x_ref.shape
    ky_count, kz_count = maps_ref.shape[-2:]
    half = kz_ref.shape[1] // 2
    depth = sources * stride
    step = pl.program_id(0)

    @pl.when(step == 0)
    def _():
        acc[...] = jnp.zeros_like(acc) if fresh else acc_in[...]
        hybrid[...] = jnp.zeros_like(hybrid)

    wide[...] = jnp.dot(
        x_ref[...].reshape(sources * rows, packed), kz_ref[...], preferred_element_type=jnp.float32
    ).reshape(sources, rows, 2 * half)

    def place(s, _):
        base = pl.multiple_of(s * stride, stride)
        for c in range(group):
            block = wide[s, pl.ds(lines * c, lines), :]
            real, imag = block[:, :half], block[:, half:]
            hybrid[c, pl.ds(base, lines), :half] = real.astype(jnp.bfloat16)
            hybrid[c, pl.ds(base, lines), half:] = imag.astype(jnp.bfloat16)
            hybrid[c, pl.ds(depth + base, lines), :half] = (-imag).astype(jnp.bfloat16)
            hybrid[c, pl.ds(depth + base, lines), half:] = real.astype(jnp.bfloat16)
        return 0

    lax.fori_loop(0, sources, place, 0)

    def one(c, _):
        image = jnp.dot(ky_ref[...], hybrid[c], preferred_element_type=jnp.float32)
        real, imag = image[:, :kz_count], image[:, half : half + kz_count]
        map_real = maps_ref[0, c, 0].astype(jnp.float32)
        map_imag = maps_ref[1, c, 0].astype(jnp.float32)
        acc[0] += map_real * real + map_imag * imag
        acc[1] += map_real * imag - map_imag * real
        return 0

    lax.fori_loop(0, group, one, 0)

    @pl.when(step == pl.num_programs(0) - 1)
    def _():
        if last and halves == 2:
            keep_ref, send_ref = outs
            count = ky_count // 2
            mine = pl.multiple_of(me_ref[0] * count, 8)
            other = pl.multiple_of((1 - me_ref[0]) * count, 8)
            for part in range(2):
                keep_ref[part] = acc[part, pl.ds(mine, count), :]
                send_ref[part] = acc[part, pl.ds(other, count), :]
        else:
            outs[0][...] = acc[...]


def image_chunk(arrived, sensitivity, kz, ky, acc, me, group, lines, stride, first_unit, last, halves):
    sources, rows_all, packed = arrived.shape
    rows = group * lines
    units = rows_all // rows
    ky_count, kz_count = sensitivity.shape[-2:]
    half = kz.shape[1] // 2
    in_specs = [
        pl.BlockSpec((sources, rows, packed), lambda i, me: (0, i, 0)),
        pl.BlockSpec((2, group, 1, ky_count, kz_count), lambda i, me: (0, i + first_unit, 0, 0, 0)),
        pl.BlockSpec(kz.shape, lambda i, me: (0, 0)),
        pl.BlockSpec(ky.shape, lambda i, me: (0, 0)),
    ]
    operands = [arrived, sensitivity, kz, ky]
    if acc is not None:
        in_specs.append(pl.BlockSpec(acc.shape, lambda i, me: (0, 0, 0)))
        operands.append(acc)
    image_shape = (2, ky_count, kz_count)
    shapes = [(2, ky_count // 2, kz_count)] * 2 if last and halves == 2 else [image_shape]
    flops = 2 * units * (sources * rows * packed * 2 * half + group * ky_count * ky.shape[1] * 2 * half)
    return pl.pallas_call(
        functools.partial(image_kernel, group, lines, stride, acc is None, last, halves),
        out_shape=[jax.ShapeDtypeStruct(s, jnp.float32) for s in shapes],
        grid_spec=pltpu.PrefetchScalarGridSpec(
            num_scalar_prefetch=1,
            grid=(units,),
            in_specs=in_specs,
            out_specs=[pl.BlockSpec(s, lambda i, me: (0, 0, 0)) for s in shapes],
            scratch_shapes=[
                pltpu.VMEM((sources, rows, 2 * half), jnp.float32),
                pltpu.VMEM((group, 2 * sources * stride, 2 * half), jnp.bfloat16),
                pltpu.VMEM(image_shape, jnp.float32),
            ],
        ),
        compiler_params=pltpu.CompilerParams(vmem_limit_bytes=VMEM_BYTES),
        cost_estimate=pl.CostEstimate(
            flops=flops, bytes_accessed=units * sources * rows * packed * 4, transcendentals=0
        ),
        name="image_of_coils",
    )(me, *operands)


def on_device(kspace, sensitivity, sampled, pole_y, order_y, pole_z, order_z):
    _, coils, _, lines, kz_count = kspace.shape
    sources = lax.axis_size("ro")
    halves = lax.axis_size("coil")
    ky_count = lines * sources
    half = round_up(kz_count, LANES)
    stride = round_up(lines, 16)
    group = 16 // math.gcd(lines, 16)
    units = coils // group
    total = sum(PLAN)
    plan = PLAN if units % total == 0 else (1,)
    plan = [units // sum(plan) * p for p in plan]
    first_line = (lax.axis_index("ro") * lines).reshape(1).astype(jnp.int32)
    me = lax.axis_index("coil").reshape(1).astype(jnp.int32)
    kz = kz_table(kz_count, half)
    ky = ky_table(ky_count, sources, stride)
    params = (sampled, pole_y, order_y, pole_z, order_z)

    starts = [sum(plan[:i]) for i in range(len(plan))]
    sends = [filter_chunk(kspace, first_line, params, group, s, n) for s, n in zip(starts, plan)]
    acc = None
    arrived = []
    for i, send in enumerate(sends):
        if i >= 2:
            acc = image_chunk(
                arrived[i - 2], sensitivity, kz, ky, acc, me, group, lines, stride, starts[i - 2], False, halves
            )[0]
            send, acc = lax.optimization_barrier((send, acc))
        arrived.append(lax.all_to_all(send, "ro", split_axis=0, concat_axis=0, tiled=True))
    for i in range(max(len(plan) - 2, 0), len(plan)):
        last = i == len(plan) - 1
        result = image_chunk(
            arrived[i], sensitivity, kz, ky, acc, me, group, lines, stride, starts[i], last, halves
        )
        acc = result[0]
    if halves == 2:
        keep, give = result
        image = keep + lax.ppermute(give, "coil", [(0, 1), (1, 0)])
        return image[:, None]
    return lax.psum_scatter(acc, "coil", scatter_dimension=1, tiled=True)[:, None]


def solution(mesh):
    return jax.shard_map(
        on_device,
        mesh=mesh,
        in_specs=(
            P(None, "coil", None, "ro", None),
            P(None, "coil", "ro", None, None),
            P(),
            P(),
            P(),
            P(),
            P(),
        ),
        out_specs=P(None, "ro", "coil", None),
        check_vma=False,
    )
```

```python
import functools
import math

import jax
import jax.numpy as jnp
import ml_dtypes
import numpy as np
from jax import lax
from jax.experimental import pallas as pl
from jax.experimental.pallas import tpu as pltpu
from jax.sharding import PartitionSpec as P

LANES = 128
VMEM_BYTES = 56 * 2**20
PLAN = (1, 6, 1)


def round_up(value, step):
    return (value + step - 1) // step * step


def dft_tables(length):
    index = np.arange(length, dtype=np.int64)
    product = index[:, None] * index[None, :] % length
    angle = product.astype(np.float32) * np.float32(2.0 * math.pi / length)
    factor = np.float32(1.0 / math.sqrt(length))
    return (
        (np.cos(angle) * factor).astype(ml_dtypes.bfloat16).astype(np.float32),
        (np.sin(angle) * factor).astype(ml_dtypes.bfloat16).astype(np.float32),
    )


def kz_table(length):
    cosine, sine = dft_tables(length)
    table = np.block([[cosine, -sine], [sine, cosine]])
    return jnp.asarray(table.astype(ml_dtypes.bfloat16))


def ky_table(length, width, groups, stride):
    lines = length // groups

    def padded(part):
        table = np.zeros((groups, stride, width), np.float32)
        table[:, :lines, :length] = part.T.reshape(groups, lines, length)
        return table.reshape(groups * stride, width)

    cosine, sine = (padded(part) for part in dft_tables(length))
    table = np.block([[cosine, sine], [-sine, cosine]])
    return jnp.asarray(table.astype(ml_dtypes.bfloat16))


def growth(frequency, pole, order):
    quotient = frequency / pole
    square = quotient * quotient
    fourth = square * square
    return 1.0 + jnp.where(order < 1.5, square, jnp.where(order < 2.5, fourth, fourth * square))


def fold(index, length):
    return jnp.minimum(index, length - index).astype(jnp.float32)


def filter_kernel(
    first_ref, x_ref, sampled_ref, pole_y_ref, order_y_ref, pole_z_ref, order_z_ref, o_ref, weight, packed
):
    _, group, lines, readouts, kz_count = x_ref.shape
    ky_count = sampled_ref.shape[-1]
    rows = group * lines
    tiles = packed.shape[0]

    @pl.when(pl.program_id(0) == 0)
    def _():
        first = first_ref[0]
        width = round_up(lines, LANES)
        line = lax.broadcasted_iota(jnp.int32, (ky_count, width), 1) + first
        place = lax.broadcasted_iota(jnp.int32, (ky_count, width), 0)
        pick = (line == place).astype(jnp.bfloat16)

        def mine(ref):
            return jnp.dot(
                ref[...].astype(jnp.float32).astype(jnp.bfloat16), pick, preferred_element_type=jnp.float32
            )

        sampled, pole_z, order_z = mine(sampled_ref), mine(pole_z_ref), mine(order_z_ref)
        pole_y = pole_y_ref[...].astype(jnp.float32)
        order_y = order_y_ref[...].astype(jnp.float32)
        freq_z = fold(lax.broadcasted_iota(jnp.int32, (readouts, kz_count), 1), kz_count)
        for k in range(lines):
            freq_y = fold(jnp.full((readouts, kz_count), first + k, jnp.int32), ky_count)
            column_y = growth(freq_y, pole_y, order_y)
            column_z = growth(freq_z, pole_z[:, k : k + 1], order_z[:, k : k + 1])
            weight[k] = sampled[:, k : k + 1] / (column_y * column_z)

    def one(k, _):
        w = weight[k]
        for c in range(group):
            at = pl.ds(pl.multiple_of((c * lines + k) * readouts, 16), readouts)
            line = jnp.concatenate([x_ref[part, c, k].astype(jnp.float32) * w for part in range(2)], axis=1)
            for t in range(tiles):
                packed[t, at, :] = line[:, t * LANES : (t + 1) * LANES]
        return 0

    lax.fori_loop(0, lines, one, 0, unroll=2)
    for t in range(tiles):
        for r in range(readouts):
            o_ref[r, :, t * LANES : (t + 1) * LANES] = packed[t, pl.ds(r, rows, stride=readouts), :].astype(
                jnp.bfloat16
            )


def filter_chunk(lines_first, first_line, params, group, first_unit, units):
    _, _, lines, readouts, kz_count = lines_first.shape
    rows = group * lines
    whole = [pl.BlockSpec(p.shape, lambda i, first: (0, 0)) for p in params]
    return pl.pallas_call(
        filter_kernel,
        out_shape=jax.ShapeDtypeStruct((readouts, units * rows, 2 * kz_count), jnp.bfloat16),
        grid_spec=pltpu.PrefetchScalarGridSpec(
            num_scalar_prefetch=1,
            grid=(units,),
            in_specs=[
                pl.BlockSpec((2, group, lines, readouts, kz_count), lambda i, first: (0, i + first_unit, 0, 0, 0)),
                *whole,
            ],
            out_specs=pl.BlockSpec((readouts, rows, 2 * kz_count), lambda i, first: (0, i, 0)),
            scratch_shapes=[
                pltpu.VMEM((lines, readouts, kz_count), jnp.float32),
                pltpu.VMEM((2 * kz_count // LANES, rows * readouts, LANES), jnp.float32),
            ],
        ),
        compiler_params=pltpu.CompilerParams(vmem_limit_bytes=VMEM_BYTES),
        cost_estimate=pl.CostEstimate(
            flops=0, bytes_accessed=5 * units * readouts * rows * 2 * kz_count, transcendentals=0
        ),
        name="window_lines",
    )(first_line, lines_first, *params)


def image_kernel(fresh, last, halves, lines, me_ref, x_ref, maps_ref, kz_ref, ky_ref, *refs):
    refs = list(refs)
    acc_in = None if fresh else refs.pop(0)
    outs, (wide, by_coil, hybrid, acc) = refs[:-4], refs[-4:]
    sources = x_ref.shape[0]
    kz_count, ky_count = maps_ref.shape[-2:]
    group, depth, _ = by_coil.shape
    stride = depth // sources
    width = ky_ref.shape[1] // 2
    step = pl.program_id(0)

    @pl.when(step == 0)
    def _():
        acc[...] = jnp.zeros_like(acc) if fresh else acc_in[...]
        by_coil[...] = jnp.zeros_like(by_coil)

    def place(s, _):
        wide[...] = x_ref[s].astype(jnp.float32)
        base = pl.multiple_of(s * stride, stride)
        for c in range(group):
            by_coil[c, pl.ds(base, lines), :] = wide[pl.ds(lines * c, lines), :].astype(jnp.bfloat16)
        return 0

    lax.fori_loop(0, sources, place, 0)

    for c in range(group):
        mixed = lax.dot_general(
            kz_ref[...], by_coil[c], (((1,), (1,)), ((), ())), preferred_element_type=jnp.float32
        )
        hybrid[c, :, :depth] = mixed[:kz_count].astype(jnp.bfloat16)
        hybrid[c, :, depth:] = mixed[kz_count:].astype(jnp.bfloat16)
    for c in range(group):
        image = jnp.dot(hybrid[c], ky_ref[...], preferred_element_type=jnp.float32)
        real, imag = image[:, :ky_count], image[:, width : width + ky_count]
        map_real = maps_ref[0, c, 0].astype(jnp.float32)
        map_imag = maps_ref[1, c, 0].astype(jnp.float32)
        acc[0] += map_real * real + map_imag * imag
        acc[1] += map_real * imag - map_imag * real

    @pl.when(step == pl.num_programs(0) - 1)
    def _():
        if last and halves == 2:
            keep_ref, send_ref = outs
            count = ky_count // 2
            lower = me_ref[0] == 0
            for part in range(2):
                low, high = acc[part, :, :count], acc[part, :, count:]
                keep_ref[part] = jnp.where(lower, low, high)
                send_ref[part] = jnp.where(lower, high, low).astype(send_ref.dtype)
        else:
            outs[0][...] = acc[...]


def image_chunk(arrived, maps, kz, ky, acc, me, group, lines, stride, first_unit, last, halves):
    sources, rows_all, packed = arrived.shape
    rows = group * lines
    units = rows_all // rows
    kz_count, ky_count = maps.shape[-2:]
    depth = sources * stride
    in_specs = [
        pl.BlockSpec((sources, rows, packed), lambda i, me: (0, i, 0)),
        pl.BlockSpec((2, group, 1, kz_count, ky_count), lambda i, me: (0, i + first_unit, 0, 0, 0)),
        pl.BlockSpec(kz.shape, lambda i, me: (0, 0)),
        pl.BlockSpec(ky.shape, lambda i, me: (0, 0)),
    ]
    operands = [arrived, maps, kz, ky]
    if acc is not None:
        in_specs.append(pl.BlockSpec(acc.shape, lambda i, me: (0, 0, 0)))
        operands.append(acc)
    image_shape = (2, kz_count, ky_count)
    outs = [jax.ShapeDtypeStruct(image_shape, jnp.float32)]
    if last and halves == 2:
        half_shape = (2, kz_count, ky_count // 2)
        outs = [jax.ShapeDtypeStruct(half_shape, jnp.float32), jax.ShapeDtypeStruct(half_shape, jnp.bfloat16)]
    flops = 2 * units * group * (packed * packed * depth + kz_count * ky.shape[0] * ky.shape[1])
    return pl.pallas_call(
        functools.partial(image_kernel, acc is None, last, halves, lines),
        out_shape=outs,
        grid_spec=pltpu.PrefetchScalarGridSpec(
            num_scalar_prefetch=1,
            grid=(units,),
            in_specs=in_specs,
            out_specs=[pl.BlockSpec(o.shape, lambda i, me: (0, 0, 0)) for o in outs],
            scratch_shapes=[
                pltpu.VMEM((rows, packed), jnp.float32),
                pltpu.VMEM((group, depth, packed), jnp.bfloat16),
                pltpu.VMEM((group, kz_count, 2 * depth), jnp.bfloat16),
                pltpu.VMEM(image_shape, jnp.float32),
            ],
        ),
        compiler_params=pltpu.CompilerParams(vmem_limit_bytes=VMEM_BYTES),
        cost_estimate=pl.CostEstimate(
            flops=flops, bytes_accessed=units * sources * rows * packed * 4, transcendentals=0
        ),
        name="image_of_coils",
    )(me, *operands)


def on_device(kspace, sensitivity, sampled, pole_y, order_y, pole_z, order_z):
    _, coils, _, lines, kz_count = kspace.shape
    sources = lax.axis_size("ro")
    halves = lax.axis_size("coil")
    ky_count = lines * sources
    stride = round_up(lines, 16)
    group = 16 // math.gcd(lines, 16)
    units = coils // group
    total = sum(PLAN)
    plan = PLAN if units % total == 0 else (1,)
    plan = [units // sum(plan) * p for p in plan]
    first_line = (lax.axis_index("ro") * lines).reshape(1).astype(jnp.int32)
    me = lax.axis_index("coil").reshape(1).astype(jnp.int32)
    kz = kz_table(kz_count)
    ky = ky_table(ky_count, round_up(ky_count, LANES), sources, stride)
    lines_first = jnp.swapaxes(kspace, 2, 3)
    maps = jnp.swapaxes(sensitivity, 3, 4)
    params = (sampled, pole_y, order_y, pole_z, order_z)

    starts = [sum(plan[:i]) for i in range(len(plan))]
    sends = [filter_chunk(lines_first, first_line, params, group, s, n) for s, n in zip(starts, plan)]
    acc = None
    arrived = []
    for i, send in enumerate(sends):
        if i >= 2:
            acc = image_chunk(
                arrived[i - 2], maps, kz, ky, acc, me, group, lines, stride, starts[i - 2], False, halves
            )[0]
            send, acc = lax.optimization_barrier((send, acc))
        arrived.append(lax.all_to_all(send, "ro", split_axis=0, concat_axis=0, tiled=True))
    for i in range(max(len(plan) - 2, 0), len(plan)):
        last = i == len(plan) - 1
        result = image_chunk(
            arrived[i], maps, kz, ky, acc, me, group, lines, stride, starts[i], last, halves
        )
        acc = result[0]
    if halves == 2:
        keep, give = result
        image = keep + lax.ppermute(give, "coil", [(0, 1), (1, 0)]).astype(jnp.float32)
    else:
        image = lax.psum_scatter(acc, "coil", scatter_dimension=2, tiled=True)
    return jnp.swapaxes(image, 1, 2)[:, None]


def solution(mesh):
    return jax.shard_map(
        on_device,
        mesh=mesh,
        in_specs=(
            P(None, "coil", None, "ro", None),
            P(None, "coil", "ro", None, None),
            P(),
            P(),
            P(),
            P(),
            P(),
        ),
        out_specs=P(None, "ro", "coil", None),
        check_vma=False,
    )
```

```python
import functools
import math

import jax
import jax.numpy as jnp
import ml_dtypes
import numpy as np
from jax import lax
from jax.experimental import pallas as pl
from jax.experimental.pallas import tpu as pltpu
from jax.sharding import PartitionSpec as P

LANES = 128
VMEM_BYTES = 56 * 2**20
FIRST, LATER = (4, 12), (12, 4)
SLOTS = 96


def round_up(value, step):
    return (value + step - 1) // step * step


def dft_tables(length):
    index = np.arange(length, dtype=np.int64)
    product = index[:, None] * index[None, :] % length
    angle = product.astype(np.float32) * np.float32(2.0 * math.pi / length)
    factor = np.float32(1.0 / math.sqrt(length))
    return (
        (np.cos(angle) * factor).astype(ml_dtypes.bfloat16).astype(np.float32),
        (np.sin(angle) * factor).astype(ml_dtypes.bfloat16).astype(np.float32),
    )


def kz_table(length):
    cosine, sine = dft_tables(length)
    table = np.block([[cosine, -sine], [sine, cosine]])
    return jnp.asarray(table.astype(ml_dtypes.bfloat16))


def ky_tables(length, width):
    def padded(part):
        table = np.zeros((length, width), np.float32)
        table[:, :length] = part.T
        return table

    cosine, sine = (padded(part) for part in dft_tables(length))
    table = np.stack([np.concatenate([cosine, sine], axis=1), np.concatenate([-sine, cosine], axis=1)])
    return jnp.asarray(table.astype(ml_dtypes.bfloat16))


def growth(quotient, order):
    square = quotient * quotient
    fourth = square * square
    return 1.0 + jnp.where(order < 1.5, square, jnp.where(order < 2.5, fourth, fourth * square))


def fold(index, length):
    return jnp.minimum(index, length - index).astype(jnp.float32)


def fill_weights(first, sampled_ref, pole_y_ref, order_y_ref, pole_z_ref, order_z_ref, weight):
    lines, readouts, kz_count = weight.shape
    ky_count = sampled_ref.shape[-1]
    width = round_up(lines, LANES)
    line = lax.broadcasted_iota(jnp.int32, (ky_count, width), 1) + first
    place = lax.broadcasted_iota(jnp.int32, (ky_count, width), 0)
    pick = (line == place).astype(jnp.bfloat16)

    def mine(ref):
        return jnp.dot(
            ref[...].astype(jnp.float32).astype(jnp.bfloat16), pick, preferred_element_type=jnp.float32
        )

    sampled, pole_z, order_z = mine(sampled_ref), mine(pole_z_ref), mine(order_z_ref)
    per_y = 1.0 / pole_y_ref[...].astype(jnp.float32)
    per_z = 1.0 / pole_z
    order_y = order_y_ref[...].astype(jnp.float32)
    freq_z = fold(lax.broadcasted_iota(jnp.int32, (readouts, kz_count), 1), kz_count)
    for k in range(lines):
        freq_y = fold(jnp.full((readouts, kz_count), first + k, jnp.int32), ky_count)
        column_y = growth(freq_y * per_y, order_y)
        column_z = growth(freq_z * per_z[:, k : k + 1], order_z[:, k : k + 1])
        weight[k] = sampled[:, k : k + 1] / (column_y * column_z)


def fill_lines(x_ref, weight, packed, coils):
    _, _, lines, readouts, _ = x_ref.shape

    def one(k, _):
        w = weight[k]
        for n, c in enumerate(coils):
            at = pl.ds(pl.multiple_of((n * lines + k) * readouts, 16), readouts)
            line = jnp.concatenate([x_ref[part, c, k].astype(jnp.float32) * w for part in range(2)], axis=1)
            for t in range(packed.shape[0]):
                packed[t, at, :] = line[:, t * LANES : (t + 1) * LANES]
        return 0

    lax.fori_loop(0, lines, one, 0, unroll=4 if lines % 4 == 0 else 2)


def window_kernel(planes, me_ref, x_ref, *refs):
    params, refs = refs[:5], refs[5:]
    outs, (weight, packed) = refs[:-2], refs[-2:]
    _, group, lines, readouts, _ = x_ref.shape

    @pl.when(pl.program_id(0) == 0)
    def _():
        fill_weights(me_ref[1] * lines, *params, weight)

    fill_lines(x_ref, weight, packed, range(group))
    for r in range(readouts):
        k = r % 4 if planes else 0
        readout = r - k + (me_ref[3] ^ k) if planes else r
        o_ref = outs[0].at[r]
        if planes:
            o_ref = outs[k].at[r // 4] if k < 2 else outs[2].at[k - 2, r // 4]
        for t in range(packed.shape[0]):
            o_ref[:, t * LANES : (t + 1) * LANES] = packed[
                t, pl.ds(readout, group * lines, stride=readouts), :
            ].astype(jnp.bfloat16)


def window_chunk(lines_first, me, params, group, planes, start, coils):
    _, _, lines, readouts, kz_count = lines_first.shape
    rows = group * lines
    tail = (coils * lines, 2 * kz_count)
    whole = [pl.BlockSpec(p.shape, lambda i, me: (0, 0)) for p in params]
    heads = [(planes,), (planes,), (2, planes)] if planes else [(readouts,)]
    return pl.pallas_call(
        functools.partial(window_kernel, planes),
        out_shape=[jax.ShapeDtypeStruct((*h, *tail), jnp.bfloat16) for h in heads],
        grid_spec=pltpu.PrefetchScalarGridSpec(
            num_scalar_prefetch=1,
            grid=(coils // group,),
            in_specs=[
                pl.BlockSpec(
                    (2, group, lines, readouts, kz_count), lambda i, me: (0, i + start // group, 0, 0, 0)
                ),
                *whole,
            ],
            out_specs=[
                pl.BlockSpec((*h, rows, tail[1]), lambda i, me, h=h: (*(0 for _ in h), i, 0)) for h in heads
            ],
            scratch_shapes=[
                pltpu.VMEM((lines, readouts, kz_count), jnp.float32),
                pltpu.VMEM((2 * kz_count // LANES, rows * readouts, LANES), jnp.float32),
            ],
        ),
        compiler_params=pltpu.CompilerParams(vmem_limit_bytes=VMEM_BYTES),
        name="window_lines",
    )(me, lines_first, *params)


def one_hot(slots, count):
    row = lax.broadcasted_iota(jnp.int32, (count, slots.shape[-1]), 0).astype(jnp.float32)
    return (row == slots).astype(jnp.bfloat16)


def pack_kernel(by_owner, me_ref, slots_ref, *refs):
    xs, (o_ref, picks) = refs[:-2], refs[-2:]
    outer, group, count, _ = o_ref.shape
    place, plane, within = me_ref[1], me_ref[2], me_ref[3]
    inner = slots_ref.shape[1] // outer

    def piece(p, k):
        if by_owner:
            return p * inner + k, place
        return p * inner + within, plane * inner + (within ^ k)

    @pl.when(pl.program_id(0) == 0)
    def _():
        for p in range(outer):
            for c in range(group):
                slots = [slots_ref[c, *piece(p, k)] for k in range(inner)]
                picks[p, c] = one_hot(jnp.concatenate(slots, axis=1), count)

    for p in range(outer):
        blocks = [xs[0][p * inner + k] for k in range(inner)] if by_owner else [x[p] for x in xs]
        lines = jnp.concatenate(blocks, axis=0)
        for c in range(group):
            o_ref[p, c] = jnp.dot(picks[p, c], lines, preferred_element_type=jnp.float32).astype(jnp.bfloat16)


def block_specs(arrays, rows):
    return [
        pl.BlockSpec((x.shape[0], rows, x.shape[2]), lambda i, me: (0, i, 0))
        if x.ndim == 3
        else pl.BlockSpec((None, x.shape[1], rows, x.shape[3]), lambda i, me: (0, 0, i, 0))
        for x in arrays
    ]


def pack_lines(held, slots, me, outer, count):
    rows_all, packed = held[0].shape[-2:]
    group, rows = slots.shape[0], slots.shape[-1]
    coils = rows_all // rows * group
    return pl.pallas_call(
        functools.partial(pack_kernel, len(held) == 1),
        out_shape=jax.ShapeDtypeStruct((outer, coils, count, packed), jnp.bfloat16),
        grid_spec=pltpu.PrefetchScalarGridSpec(
            num_scalar_prefetch=1,
            grid=(coils // group,),
            in_specs=[pl.BlockSpec(slots.shape, lambda i, me: (0,) * slots.ndim), *block_specs(held, rows)],
            out_specs=pl.BlockSpec((outer, group, count, packed), lambda i, me: (0, i, 0, 0)),
            scratch_shapes=[pltpu.VMEM((outer, group, count, slots.shape[1] // outer * rows), jnp.bfloat16)],
        ),
        compiler_params=pltpu.CompilerParams(vmem_limit_bytes=VMEM_BYTES),
        name="pack_sampled",
    )(me, slots, *held)


def unpack_kernel(me_ref, slots_ref, x_ref, own_ref, first_ref, others_ref, places):
    outer, group, count, packed = x_ref.shape
    inner, rows = places.shape[1], places.shape[2]
    plane, within = me_ref[2], me_ref[3]

    @pl.when(pl.program_id(0) == 0)
    def _():
        for p in range(outer):
            for k in range(inner):
                row = jnp.full((1, rows), -1.0, jnp.float32)
                for c in range(group):
                    slots = slots_ref[c, plane * inner + (within ^ k), p * inner + within]
                    held = jnp.logical_and(slots >= 0, slots < count)
                    row = jnp.where(held, slots + c * count, row)
                row = jnp.concatenate([row, jnp.full((1, -rows % LANES), -1.0, jnp.float32)], axis=1)
                spread = one_hot(row, group * count).astype(jnp.float32).T
                places[p, k] = spread[:rows].astype(jnp.bfloat16)

    for p in range(outer):
        held = x_ref[p].reshape(group * count, packed)
        for k in range(inner):
            out = own_ref.at[p] if k == 0 else first_ref.at[p] if k == 1 else others_ref.at[k - 2, p]
            out[...] = jnp.dot(places[p, k], held, preferred_element_type=jnp.float32).astype(jnp.bfloat16)


def unpack_lines(arrived, slots, me):
    outer, coils, count, packed = arrived.shape
    group, rows = slots.shape[0], slots.shape[-1]
    tail = (coils // group * rows, packed)
    heads = [(outer,), (outer,), (2, outer)]
    return pl.pallas_call(
        unpack_kernel,
        out_shape=[jax.ShapeDtypeStruct((*h, *tail), jnp.bfloat16) for h in heads],
        grid_spec=pltpu.PrefetchScalarGridSpec(
            num_scalar_prefetch=1,
            grid=(coils // group,),
            in_specs=[
                pl.BlockSpec(slots.shape, lambda i, me: (0,) * slots.ndim),
                pl.BlockSpec((outer, group, count, packed), lambda i, me: (0, i, 0, 0)),
            ],
            out_specs=[
                pl.BlockSpec((*h, rows, packed), lambda i, me, h=h: (*(0 for _ in h), i, 0)) for h in heads
            ],
            scratch_shapes=[pltpu.VMEM((outer, slots.shape[1] // outer, rows, group * count), jnp.bfloat16)],
        ),
        compiler_params=pltpu.CompilerParams(vmem_limit_bytes=VMEM_BYTES),
        name="unpack_sampled",
    )(me, slots, arrived)


def pick_kernel(count, me_ref, slots_ref, table_ref, o_ref):
    o_ref[...] = jnp.zeros_like(o_ref)
    for p in range(slots_ref.shape[1]):
        pick = one_hot(slots_ref[me_ref[1], p], count)
        for part in range(2):
            o_ref[part, pl.ds(p * count, count), :] = jnp.dot(
                pick, table_ref[part, p], preferred_element_type=jnp.float32
            ).astype(jnp.bfloat16)


def pick_rows(table, slots, me, count, depth):
    outer = slots.shape[1]
    table = table.reshape(2, outer, table.shape[1] // outer, table.shape[2])
    shape = (2, depth, table.shape[3])
    return pl.pallas_call(
        functools.partial(pick_kernel, count),
        out_shape=jax.ShapeDtypeStruct(shape, jnp.bfloat16),
        grid_spec=pltpu.PrefetchScalarGridSpec(
            num_scalar_prefetch=1,
            grid=(1,),
            in_specs=[
                pl.BlockSpec(slots.shape, lambda i, me: (0, 0, 0, 0)),
                pl.BlockSpec(table.shape, lambda i, me: (0, 0, 0, 0)),
            ],
            out_specs=pl.BlockSpec(shape, lambda i, me: (0, 0, 0)),
        ),
        compiler_params=pltpu.CompilerParams(vmem_limit_bytes=VMEM_BYTES),
        name="pick_table_rows",
    )(me, slots, table)


def image_kernel(fresh, last, halves, lines, group, pieces, me_ref, *refs):
    xs, refs = refs[:pieces], list(refs[pieces:])
    x_ref, (maps_ref, kz_ref, ky_ref), refs = xs[0], refs[:3], refs[3:]
    acc_in = None if fresh else refs.pop(0)
    outs, (wide, by_line, hybrid, acc) = refs[:-4], refs[-4:]
    kz_count, ky_count = maps_ref.shape[-2:]
    depth = by_line.shape[1]
    width = ky_ref.shape[-1] // 2
    step = pl.program_id(0)

    @pl.when(step == 0)
    def _():
        acc[...] = jnp.zeros_like(acc) if fresh else acc_in[...]
        by_line[...] = jnp.zeros_like(by_line)

    if lines:
        stride = depth // (x_ref.shape[0] * pieces)

        for k in range(pieces):

            def place(s, _, k=k):
                wide[k % 2] = xs[k][s].astype(jnp.float32)
                source = s * pieces + (me_ref[3] ^ k) if pieces > 1 else s
                base = pl.multiple_of(source * stride, stride)
                for c in range(group):
                    by_line[c, pl.ds(base, lines), :] = wide[k % 2, pl.ds(lines * c, lines), :].astype(jnp.bfloat16)
                return 0

            lax.fori_loop(0, x_ref.shape[0], place, 0)
    else:
        count = x_ref.shape[2]
        for c in range(group):
            for p in range(x_ref.shape[0]):
                by_line[c, p * count : (p + 1) * count, :] = x_ref[p, c]

    for c in range(group):
        mixed = lax.dot_general(
            kz_ref[...], by_line[c], (((1,), (1,)), ((), ())), preferred_element_type=jnp.float32
        )
        hybrid[c, :, :depth] = mixed[:kz_count].astype(jnp.bfloat16)
        hybrid[c, :, depth:] = mixed[kz_count:].astype(jnp.bfloat16)
    for c in range(group):
        image = jnp.dot(
            hybrid[c], ky_ref[...].reshape(2 * depth, 2 * width), preferred_element_type=jnp.float32
        )
        real, imag = image[:, :ky_count], image[:, width : width + ky_count]
        map_real = maps_ref[0, c, 0].astype(jnp.float32)
        map_imag = maps_ref[1, c, 0].astype(jnp.float32)
        acc[0] += map_real * real + map_imag * imag
        acc[1] += map_real * imag - map_imag * real

    @pl.when(step == pl.num_programs(0) - 1)
    def _():
        if last and halves == 2:
            keep_ref, send_ref = outs
            rows = ky_count // 2
            lower = me_ref[0] == 0
            for part in range(2):
                low, high = acc[part, :, :rows], acc[part, :, rows:]
                keep_ref[part] = jnp.where(lower, low, high)
                send_ref[part] = jnp.where(lower, high, low).astype(send_ref.dtype)
        else:
            outs[0][...] = acc[...]


def image_chunk(arrived, maps, kz, ky, acc, me, group, lines, start, coils, last, halves):
    kz_count, ky_count = maps.shape[-2:]
    packed = arrived[0].shape[-1]
    depth = ky.shape[1]
    if lines:
        x_specs = block_specs(arrived, group * lines)
    else:
        group = 2
        x_specs = [
            pl.BlockSpec((x.shape[0], group, *x.shape[2:]), lambda i, me: (0, i, 0, 0)) for x in arrived
        ]
    wide = (2, max(group * lines, 8), packed)
    in_specs = [
        *x_specs,
        pl.BlockSpec((2, group, 1, kz_count, ky_count), lambda i, me: (0, i + start // group, 0, 0, 0)),
        pl.BlockSpec(kz.shape, lambda i, me: (0, 0)),
        pl.BlockSpec(ky.shape, lambda i, me: (0, 0, 0)),
    ]
    operands = [*arrived, maps, kz, ky]
    if acc is not None:
        in_specs.append(pl.BlockSpec(acc.shape, lambda i, me: (0, 0, 0)))
        operands.append(acc)
    image_shape = (2, kz_count, ky_count)
    outs = [jax.ShapeDtypeStruct(image_shape, jnp.float32)]
    if last and halves == 2:
        half_shape = (2, kz_count, ky_count // 2)
        outs = [jax.ShapeDtypeStruct(half_shape, jnp.float32), jax.ShapeDtypeStruct(half_shape, jnp.bfloat16)]
    return pl.pallas_call(
        functools.partial(image_kernel, acc is None, last, halves, lines, group, len(arrived)),
        out_shape=outs,
        grid_spec=pltpu.PrefetchScalarGridSpec(
            num_scalar_prefetch=1,
            grid=(coils // group,),
            in_specs=in_specs,
            out_specs=[pl.BlockSpec(o.shape, lambda i, me: (0, 0, 0)) for o in outs],
            scratch_shapes=[
                pltpu.VMEM(wide, jnp.float32),
                pltpu.VMEM((group, depth, packed), jnp.bfloat16),
                pltpu.VMEM((group, kz_count, 2 * depth), jnp.bfloat16),
                pltpu.VMEM(image_shape, jnp.float32),
            ],
        ),
        compiler_params=pltpu.CompilerParams(vmem_limit_bytes=VMEM_BYTES),
        name="image_of_coils",
    )(me, *operands)


def ranks(taken):
    lines = taken.shape[-1]
    before = jnp.asarray(np.triu(np.ones((lines, lines), np.float32), 1).astype(ml_dtypes.bfloat16))
    flat = taken.reshape(-1, lines).astype(jnp.bfloat16)
    rank = jnp.dot(flat, before, preferred_element_type=jnp.float32)
    return jnp.where(flat > 0, rank, -1.0).reshape(taken.shape)


def on_device(kspace, sensitivity, sampled, pole_y, order_y, pole_z, order_z):
    _, coils, readouts, lines, kz_count = kspace.shape
    devices = lax.axis_size("ro")
    halves = lax.axis_size("coil")
    ky_count = lines * devices
    stride = round_up(lines, 16)
    inner = 16 // math.gcd(lines, 16)
    outer = devices // inner
    parts = [(coils,), ()] if inner != 4 or coils != sum(FIRST + LATER) else [FIRST, LATER]
    planned = len(parts[1]) > 0
    place = lax.axis_index("ro")
    me = jnp.stack([lax.axis_index("coil"), place, place // inner, place % inner]).astype(jnp.int32)
    lines_first = jnp.swapaxes(kspace, 2, 3)
    maps = jnp.swapaxes(sensitivity, 3, 4)
    params = (sampled, pole_y, order_y, pole_z, order_z)
    kz = kz_table(kz_count)
    tables = ky_tables(ky_count, round_up(ky_count, LANES))
    ky = jnp.pad(tables.reshape(2, devices, lines, -1), ((0, 0), (0, 0), (0, stride - lines), (0, 0))).reshape(
        2, devices * stride, -1
    )

    def window(planes, start, count):
        return window_chunk(lines_first, me, params, inner, planes, start, count)

    def image(arrived, rows, by_line, start, count, acc, last=False):
        return image_chunk(
            arrived, maps, kz, rows, acc, me, inner, lines if by_line else 0, start, count, last, halves
        )

    def to_place(array, k):
        return lax.ppermute(array, "ro", [(a, a ^ k) for a in range(devices)])

    def in_plane(own, first, others):
        across = to_place(others, 2)
        return [own, to_place(first, 1), across, to_place(across[1], 1)]

    def to_planes(packed):
        same_place = [[p * inner + i for p in range(outer)] for i in range(inner)]
        return lax.all_to_all(
            packed, "ro", split_axis=0, concat_axis=0, tiled=True, axis_index_groups=same_place
        )

    def apart(slots):
        return jnp.stack(
            [
                jnp.pad(
                    slots[:, :, None],
                    ((0, 0), (0, 0), (0, 0), (c * lines, (inner - 1 - c) * lines)),
                    constant_values=-1,
                )
                for c in range(inner)
            ]
        )

    def finish(result):
        if halves == 2:
            keep, give = result
            whole = keep + lax.ppermute(give, "coil", [(0, 1), (1, 0)]).astype(jnp.float32)
        else:
            whole = lax.psum_scatter(result[0], "coil", scatter_dimension=2, tiled=True)
        return jnp.swapaxes(whole, 1, 2)[:, None]

    if not planned:
        sent = window(0, 0, coils)[0]
        arrived = lax.all_to_all(sent, "ro", split_axis=0, concat_axis=0, tiled=True)
        return finish(image([arrived], ky, True, 0, coils, None, True))

    by_source = jnp.swapaxes(sampled.reshape(outer, inner, devices, lines), 1, 2)
    source_slots = jnp.swapaxes(ranks(by_source.reshape(outer, devices, -1)).reshape(by_source.shape), 1, 2)
    source_slots = source_slots.reshape(readouts, devices, lines)
    by_plane = sampled.reshape(readouts, outer, inner * lines)
    plane_slots = ranks(by_plane)
    counts = [jnp.sum(by_source, axis=(2, 3)), jnp.sum(by_plane, axis=2)]

    def slot_arrays(first_slot):
        return (
            apart(source_slots - first_slot),
            apart((plane_slots - first_slot).reshape(readouts, devices, lines)),
            (plane_slots - first_slot)[:, :, None],
        )

    starts = [sum((FIRST + LATER)[:i]) for i in range(len(FIRST + LATER))]
    first_starts, later_starts = starts[: len(FIRST)], starts[len(FIRST) :]
    for_source, for_plane, for_rows = slot_arrays(0)
    rows = pick_rows(tables, for_rows, me, SLOTS, round_up(outer * SLOTS, LANES))

    windowed = [window(0, start, count) for start, count in zip(first_starts, FIRST)]
    later = [window(outer, start, count) for start, count in zip(later_starts, LATER)]
    packs = [pack_lines(part, for_source, me, outer, SLOTS) for part in windowed]
    crossed = [to_planes(packs[0])]
    second, crossed[0], later[0] = lax.optimization_barrier((packs[1], crossed[0], later[0]))
    crossed.append(to_planes(second))
    gathered = [in_plane(*part) for part in later]
    spread = in_plane(*unpack_lines(crossed[0], for_source, me))
    acc = image(spread, ky, True, first_starts[0], FIRST[0], None)[0]
    here, acc = lax.optimization_barrier((me, acc))
    third = pack_lines(gathered[0], for_plane, here, outer, SLOTS)
    third, crossed[1] = lax.optimization_barrier((third, crossed[1]))
    third = to_planes(third)
    spread = in_plane(*unpack_lines(crossed[1], for_source, me))
    fourth = pack_lines(gathered[1], for_plane, me, outer, SLOTS)

    def rest_of_lines():
        for_source, for_plane, for_rows = slot_arrays(SLOTS)
        left = inner * lines - SLOTS
        rows = pick_rows(tables, for_rows, me, left, round_up(outer * left, LANES))
        total = None
        for start, count, sent in zip(first_starts, FIRST, windowed):
            part = to_planes(pack_lines(sent, for_source, me, outer, left))
            total = image(in_plane(*unpack_lines(part, for_source, me)), ky, True, start, count, total)[0]
        for start, count, held in zip(later_starts, LATER, gathered):
            part = to_planes(pack_lines(held, for_plane, me, outer, left))
            total = image([part], rows, False, start, count, total)[0]
        return total

    counts, acc, third, fourth = lax.optimization_barrier((counts, acc, third, fourth))
    most = jnp.maximum(jnp.max(counts[0]), jnp.max(counts[1]))
    acc = lax.cond(most > SLOTS, lambda a: a + rest_of_lines(), lambda a: a, acc)
    fourth, acc, spread = lax.optimization_barrier((fourth, acc, spread))
    fourth = to_planes(fourth)
    acc = image(spread, ky, True, first_starts[1], FIRST[1], acc)[0]
    acc = image([third], rows, False, later_starts[0], LATER[0], acc)[0]
    return finish(image([fourth], rows, False, later_starts[1], LATER[1], acc, True))


def solution(mesh):
    return jax.shard_map(
        on_device,
        mesh=mesh,
        in_specs=(
            P(None, "coil", None, "ro", None),
            P(None, "coil", "ro", None, None),
            P(),
            P(),
            P(),
            P(),
            P(),
        ),
        out_specs=P(None, "ro", "coil", None),
        check_vma=False,
    )
```

```python
import functools
import math

import jax
import jax.numpy as jnp
import ml_dtypes
import numpy as np
from jax import lax
from jax.experimental import pallas as pl
from jax.experimental.pallas import tpu as pltpu
from jax.sharding import PartitionSpec as P

LANES = 128
VMEM_BYTES = 56 * 2**20
FIRST, LATER = (4, 12), (12, 4)
STRAIGHT = (4, 24, 4)
SLOTS = 96


def round_up(value, step):
    return (value + step - 1) // step * step


def dft_tables(length):
    index = np.arange(length, dtype=np.int64)
    product = index[:, None] * index[None, :] % length
    angle = product.astype(np.float32) * np.float32(2.0 * math.pi / length)
    factor = np.float32(1.0 / math.sqrt(length))
    return (
        (np.cos(angle) * factor).astype(ml_dtypes.bfloat16).astype(np.float32),
        (np.sin(angle) * factor).astype(ml_dtypes.bfloat16).astype(np.float32),
    )


def kz_table(length):
    cosine, sine = dft_tables(length)
    table = np.block([[cosine, -sine], [sine, cosine]])
    return jnp.asarray(table.astype(ml_dtypes.bfloat16))


def ky_tables(length, width):
    def padded(part):
        table = np.zeros((length, width), np.float32)
        table[:, :length] = part.T
        return table

    cosine, sine = (padded(part) for part in dft_tables(length))
    table = np.stack([np.concatenate([cosine, sine], axis=1), np.concatenate([-sine, cosine], axis=1)])
    return jnp.asarray(table.astype(ml_dtypes.bfloat16))


def growth(quotient, order):
    square = quotient * quotient
    fourth = square * square
    return 1.0 + jnp.where(order < 1.5, square, jnp.where(order < 2.5, fourth, fourth * square))


def fold(index, length):
    return jnp.minimum(index, length - index).astype(jnp.float32)


def fill_weights(first, sampled_ref, pole_y_ref, order_y_ref, pole_z_ref, order_z_ref, weight):
    lines, readouts, kz_count = weight.shape
    ky_count = sampled_ref.shape[-1]
    width = round_up(lines, LANES)
    line = lax.broadcasted_iota(jnp.int32, (ky_count, width), 1) + first
    place = lax.broadcasted_iota(jnp.int32, (ky_count, width), 0)
    pick = (line == place).astype(jnp.bfloat16)

    def mine(ref):
        return jnp.dot(
            ref[...].astype(jnp.float32).astype(jnp.bfloat16), pick, preferred_element_type=jnp.float32
        )

    sampled, pole_z, order_z = mine(sampled_ref), mine(pole_z_ref), mine(order_z_ref)
    per_y = 1.0 / pole_y_ref[...].astype(jnp.float32)
    per_z = 1.0 / pole_z
    order_y = order_y_ref[...].astype(jnp.float32)
    freq_z = fold(lax.broadcasted_iota(jnp.int32, (readouts, kz_count), 1), kz_count)
    for k in range(lines):
        freq_y = fold(jnp.full((readouts, kz_count), first + k, jnp.int32), ky_count)
        column_y = growth(freq_y * per_y, order_y)
        column_z = growth(freq_z * per_z[:, k : k + 1], order_z[:, k : k + 1])
        weight[k] = sampled[:, k : k + 1] / (column_y * column_z)


def fill_lines(x_ref, weight, packed, coils):
    _, _, lines, readouts, _ = x_ref.shape

    def one(k, _):
        w = weight[k]
        for n, c in enumerate(coils):
            at = pl.ds(pl.multiple_of((n * lines + k) * readouts, 16), readouts)
            line = jnp.concatenate([x_ref[part, c, k].astype(jnp.float32) * w for part in range(2)], axis=1)
            for t in range(packed.shape[0]):
                packed[t, at, :] = line[:, t * LANES : (t + 1) * LANES]
        return 0

    lax.fori_loop(0, lines, one, 0, unroll=4 if lines % 4 == 0 else 2)


def window_kernel(planes, me_ref, x_ref, *refs):
    params, refs = refs[:5], refs[5:]
    outs, (weight, packed) = refs[:-2], refs[-2:]
    _, group, lines, readouts, _ = x_ref.shape

    @pl.when(pl.program_id(0) == 0)
    def _():
        fill_weights(me_ref[1] * lines, *params, weight)

    fill_lines(x_ref, weight, packed, range(group))
    for r in range(readouts):
        k = r % 4 if planes else 0
        readout = r - k + (me_ref[3] ^ k) if planes else r
        o_ref = outs[0].at[r]
        if planes:
            o_ref = outs[k].at[r // 4] if k < 2 else outs[2].at[k - 2, r // 4]
        for t in range(packed.shape[0]):
            o_ref[:, t * LANES : (t + 1) * LANES] = packed[
                t, pl.ds(readout, group * lines, stride=readouts), :
            ].astype(jnp.bfloat16)


def window_chunk(lines_first, me, params, group, planes, start, coils):
    _, _, lines, readouts, kz_count = lines_first.shape
    rows = group * lines
    tail = (coils * lines, 2 * kz_count)
    whole = [pl.BlockSpec(p.shape, lambda i, me: (0, 0)) for p in params]
    heads = [(planes,), (planes,), (2, planes)] if planes else [(readouts,)]
    return pl.pallas_call(
        functools.partial(window_kernel, planes),
        out_shape=[jax.ShapeDtypeStruct((*h, *tail), jnp.bfloat16) for h in heads],
        grid_spec=pltpu.PrefetchScalarGridSpec(
            num_scalar_prefetch=1,
            grid=(coils // group,),
            in_specs=[
                pl.BlockSpec(
                    (2, group, lines, readouts, kz_count), lambda i, me: (0, i + start // group, 0, 0, 0)
                ),
                *whole,
            ],
            out_specs=[
                pl.BlockSpec((*h, rows, tail[1]), lambda i, me, h=h: (*(0 for _ in h), i, 0)) for h in heads
            ],
            scratch_shapes=[
                pltpu.VMEM((lines, readouts, kz_count), jnp.float32),
                pltpu.VMEM((2 * kz_count // LANES, rows * readouts, LANES), jnp.float32),
            ],
        ),
        compiler_params=pltpu.CompilerParams(vmem_limit_bytes=VMEM_BYTES),
        name="window_lines",
    )(me, lines_first, *params)


def one_hot(slots, count):
    row = lax.broadcasted_iota(jnp.int32, (count, slots.shape[-1]), 0).astype(jnp.float32)
    return (row == slots).astype(jnp.bfloat16)


def taken_lines(sampled_ref, first, lines):
    ky_count = sampled_ref.shape[-1]
    place = lax.broadcasted_iota(jnp.int32, (ky_count, LANES), 0)
    lane = lax.broadcasted_iota(jnp.int32, (ky_count, LANES), 1)
    pick = jnp.logical_and(lane + first == place, lane < lines).astype(jnp.bfloat16)
    return jnp.dot(
        sampled_ref[...].astype(jnp.float32).astype(jnp.bfloat16), pick, preferred_element_type=jnp.float32
    )


def source_slots(sampled_ref, source, lines, inner):
    taken = taken_lines(sampled_ref, source * lines, lines)
    readouts = taken.shape[0]
    row = lax.broadcasted_iota(jnp.int32, (LANES, LANES), 0)
    before = (row < lax.broadcasted_iota(jnp.int32, (LANES, LANES), 1)).astype(jnp.bfloat16)
    rank = jnp.dot(taken.astype(jnp.bfloat16), before, preferred_element_type=jnp.float32)
    owner = lax.broadcasted_iota(jnp.int32, (readouts, readouts), 0)
    other = lax.broadcasted_iota(jnp.int32, (readouts, readouts), 1)
    ahead = jnp.logical_and(owner // inner == other // inner, other < owner).astype(jnp.bfloat16)
    past = jnp.dot(ahead, taken.astype(jnp.bfloat16), preferred_element_type=jnp.float32)
    return jnp.where(taken > 0, rank + jnp.sum(past, axis=1, keepdims=True), -1.0)


def among(slots, c, group):
    empty = jnp.full_like(slots, -1.0)
    return [slots if n == c else empty for n in range(group)]


def pack_kernel(by_owner, me_ref, slots_ref, *refs):
    xs, (o_ref, picks) = refs[:-2], refs[-2:]
    outer, group, count, _ = o_ref.shape
    place, plane, within = me_ref[1], me_ref[2], me_ref[3]
    inner, rows = (xs[0].shape[0] // outer, xs[0].shape[1]) if by_owner else (len(xs), xs[0].shape[1])
    lines = rows // group

    @pl.when(pl.program_id(0) == 0)
    def _():
        if by_owner:
            own = source_slots(slots_ref, place, lines, inner)
        for p in range(outer):
            if by_owner:
                slots = [own[p * inner + k : p * inner + k + 1, :lines] for k in range(inner)]
            else:
                slots = [slots_ref[p * inner + within, plane * inner + (within ^ k)] for k in range(inner)]
            for c in range(group):
                picks[p, c] = one_hot(jnp.concatenate(sum([among(s, c, group) for s in slots], []), axis=1), count)

    for p in range(outer):
        blocks = [xs[0][p * inner + k] for k in range(inner)] if by_owner else [x[p] for x in xs]
        held = jnp.concatenate(blocks, axis=0)
        for c in range(group):
            o_ref[p, c] = jnp.dot(picks[p, c], held, preferred_element_type=jnp.float32).astype(jnp.bfloat16)


def block_specs(arrays, rows):
    return [
        pl.BlockSpec((x.shape[0], rows, x.shape[2]), lambda i, me: (0, i, 0))
        if x.ndim == 3
        else pl.BlockSpec((None, x.shape[1], rows, x.shape[3]), lambda i, me: (0, 0, i, 0))
        for x in arrays
    ]


def pack_lines(held, slots, me, outer, inner, lines, count):
    rows_all, packed = held[0].shape[-2:]
    group = inner
    rows = group * lines
    coils = rows_all // lines
    return pl.pallas_call(
        functools.partial(pack_kernel, len(held) == 1),
        out_shape=jax.ShapeDtypeStruct((outer, coils, count, packed), jnp.bfloat16),
        grid_spec=pltpu.PrefetchScalarGridSpec(
            num_scalar_prefetch=1,
            grid=(coils // group,),
            in_specs=[pl.BlockSpec(slots.shape, lambda i, me: (0,) * slots.ndim), *block_specs(held, rows)],
            out_specs=pl.BlockSpec((outer, group, count, packed), lambda i, me: (0, i, 0, 0)),
            scratch_shapes=[pltpu.VMEM((outer, group, count, inner * rows), jnp.bfloat16)],
        ),
        compiler_params=pltpu.CompilerParams(vmem_limit_bytes=VMEM_BYTES),
        name="pack_sampled",
    )(me, slots, *held)


def unpack_kernel(me_ref, sampled_ref, x_ref, own_ref, first_ref, others_ref, places, ranks):
    outer, group, count, packed = x_ref.shape
    inner, rows = places.shape[1], places.shape[2]
    lines = rows // group
    plane, within = me_ref[2], me_ref[3]

    @pl.when(pl.program_id(0) == 0)
    def _():
        for p in range(outer):
            ranks[...] = source_slots(sampled_ref, p * inner + within, lines, inner)
            for k in range(inner):
                slots = ranks[pl.ds(plane * inner + (within ^ k), 1), :][:, :lines]
                row = [jnp.where(slots >= 0, slots + c * count, -1.0) for c in range(group)]
                row = jnp.concatenate([*row, jnp.full((1, -rows % LANES), -1.0, jnp.float32)], axis=1)
                spread = one_hot(row, group * count).astype(jnp.float32).T
                places[p, k] = spread[:rows].astype(jnp.bfloat16)

    for p in range(outer):
        held = x_ref[p].reshape(group * count, packed)
        for k in range(inner):
            out = own_ref.at[p] if k == 0 else first_ref.at[p] if k == 1 else others_ref.at[k - 2, p]
            out[...] = jnp.dot(places[p, k], held, preferred_element_type=jnp.float32).astype(jnp.bfloat16)


def unpack_lines(arrived, sampled, me, inner, lines):
    outer, coils, count, packed = arrived.shape
    group = inner
    rows = group * lines
    tail = (coils * lines, packed)
    heads = [(outer,), (outer,), (2, outer)]
    return pl.pallas_call(
        unpack_kernel,
        out_shape=[jax.ShapeDtypeStruct((*h, *tail), jnp.bfloat16) for h in heads],
        grid_spec=pltpu.PrefetchScalarGridSpec(
            num_scalar_prefetch=1,
            grid=(coils // group,),
            in_specs=[
                pl.BlockSpec(sampled.shape, lambda i, me: (0, 0)),
                pl.BlockSpec((outer, group, count, packed), lambda i, me: (0, i, 0, 0)),
            ],
            out_specs=[
                pl.BlockSpec((*h, rows, packed), lambda i, me, h=h: (*(0 for _ in h), i, 0)) for h in heads
            ],
            scratch_shapes=[
                pltpu.VMEM((outer, inner, rows, group * count), jnp.bfloat16),
                pltpu.VMEM((sampled.shape[0], LANES), jnp.float32),
            ],
        ),
        compiler_params=pltpu.CompilerParams(vmem_limit_bytes=VMEM_BYTES),
        name="unpack_sampled",
    )(me, sampled, arrived)


def most_kernel(inner, outer, sampled_ref, o_ref):
    readouts, ky_count = sampled_ref.shape
    devices = inner * outer
    taken = sampled_ref[...].astype(jnp.float32).astype(jnp.bfloat16)
    line = lax.broadcasted_iota(jnp.int32, (ky_count, LANES), 0)
    lane = lax.broadcasted_iota(jnp.int32, (ky_count, LANES), 1)

    def sums(parts):
        return jnp.dot(
            taken, (line // (ky_count // parts) == lane).astype(jnp.bfloat16), preferred_element_type=jnp.float32
        )

    row = lax.broadcasted_iota(jnp.int32, (readouts, readouts), 0)
    readout = lax.broadcasted_iota(jnp.int32, (readouts, readouts), 1)
    together = (row // inner == readout // inner).astype(jnp.bfloat16)
    by_source = jnp.dot(together, sums(devices).astype(jnp.bfloat16), preferred_element_type=jnp.float32)
    o_ref[0, 0] = jnp.max(jnp.maximum(by_source, sums(outer))).astype(jnp.int32)


def most_lines(sampled, inner, outer):
    return pl.pallas_call(
        functools.partial(most_kernel, inner, outer),
        out_shape=jax.ShapeDtypeStruct((1, 1), jnp.int32),
        out_specs=pl.BlockSpec(memory_space=pltpu.SMEM),
        name="most_lines",
    )(sampled)[0, 0]


def pick_kernel(count, me_ref, slots_ref, table_ref, o_ref):
    o_ref[...] = jnp.zeros_like(o_ref)
    for p in range(slots_ref.shape[1]):
        pick = one_hot(slots_ref[me_ref[1], p], count)
        for part in range(2):
            o_ref[part, pl.ds(p * count, count), :] = jnp.dot(
                pick, table_ref[part, p], preferred_element_type=jnp.float32
            ).astype(jnp.bfloat16)


def pick_rows(table, slots, me, count, depth):
    outer = slots.shape[1]
    table = table.reshape(2, outer, table.shape[1] // outer, table.shape[2])
    shape = (2, depth, table.shape[3])
    return pl.pallas_call(
        functools.partial(pick_kernel, count),
        out_shape=jax.ShapeDtypeStruct(shape, jnp.bfloat16),
        grid_spec=pltpu.PrefetchScalarGridSpec(
            num_scalar_prefetch=1,
            grid=(1,),
            in_specs=[
                pl.BlockSpec(slots.shape, lambda i, me: (0, 0, 0, 0)),
                pl.BlockSpec(table.shape, lambda i, me: (0, 0, 0, 0)),
            ],
            out_specs=pl.BlockSpec(shape, lambda i, me: (0, 0, 0)),
        ),
        compiler_params=pltpu.CompilerParams(vmem_limit_bytes=VMEM_BYTES),
        name="pick_table_rows",
    )(me, slots, table)


def image_kernel(fresh, last, halves, lines, group, pieces, me_ref, *refs):
    xs, refs = refs[:pieces], list(refs[pieces:])
    x_ref, (maps_ref, kz_ref, ky_ref), refs = xs[0], refs[:3], refs[3:]
    acc_in = None if fresh else refs.pop(0)
    outs, (wide, by_line, hybrid, acc) = refs[:-4], refs[-4:]
    kz_count, ky_count = maps_ref.shape[-2:]
    depth = by_line.shape[1]
    width = ky_ref.shape[-1] // 2
    step = pl.program_id(0)

    @pl.when(step == 0)
    def _():
        acc[...] = jnp.zeros_like(acc) if fresh else acc_in[...]
        by_line[...] = jnp.zeros_like(by_line)

    if lines:
        stride = depth // (x_ref.shape[0] * pieces)

        for k in range(pieces):

            def place(s, _, k=k):
                wide[k % 2] = xs[k][s].astype(jnp.float32)
                source = s * pieces + (me_ref[3] ^ k) if pieces > 1 else s
                base = pl.multiple_of(source * stride, stride)
                for c in range(group):
                    by_line[c, pl.ds(base, lines), :] = wide[k % 2, pl.ds(lines * c, lines), :].astype(jnp.bfloat16)
                return 0

            lax.fori_loop(0, x_ref.shape[0], place, 0)
    else:
        count = x_ref.shape[2]
        for c in range(group):
            for p in range(x_ref.shape[0]):
                by_line[c, p * count : (p + 1) * count, :] = x_ref[p, c]

    for c in range(group):
        mixed = lax.dot_general(
            kz_ref[...], by_line[c], (((1,), (1,)), ((), ())), preferred_element_type=jnp.float32
        )
        hybrid[c, :, :depth] = mixed[:kz_count].astype(jnp.bfloat16)
        hybrid[c, :, depth:] = mixed[kz_count:].astype(jnp.bfloat16)
    for c in range(group):
        image = jnp.dot(
            hybrid[c], ky_ref[...].reshape(2 * depth, 2 * width), preferred_element_type=jnp.float32
        )
        real, imag = image[:, :ky_count], image[:, width : width + ky_count]
        map_real = maps_ref[0, c, 0].astype(jnp.float32)
        map_imag = maps_ref[1, c, 0].astype(jnp.float32)
        acc[0] += map_real * real + map_imag * imag
        acc[1] += map_real * imag - map_imag * real

    @pl.when(step == pl.num_programs(0) - 1)
    def _():
        if last and halves == 2:
            keep_ref, send_ref = outs
            rows = ky_count // 2
            lower = me_ref[0] == 0
            for part in range(2):
                low, high = acc[part, :, :rows], acc[part, :, rows:]
                keep_ref[part] = jnp.where(lower, low, high)
                send_ref[part] = jnp.where(lower, high, low).astype(send_ref.dtype)
        else:
            outs[0][...] = acc[...]


def image_chunk(arrived, maps, kz, ky, acc, me, group, lines, start, coils, last, halves):
    kz_count, ky_count = maps.shape[-2:]
    packed = arrived[0].shape[-1]
    depth = ky.shape[1]
    if lines:
        x_specs = block_specs(arrived, group * lines)
    else:
        group = 2
        x_specs = [
            pl.BlockSpec((x.shape[0], group, *x.shape[2:]), lambda i, me: (0, i, 0, 0)) for x in arrived
        ]
    wide = (2, max(group * lines, 8), packed)
    in_specs = [
        *x_specs,
        pl.BlockSpec((2, group, 1, kz_count, ky_count), lambda i, me: (0, i + start // group, 0, 0, 0)),
        pl.BlockSpec(kz.shape, lambda i, me: (0, 0)),
        pl.BlockSpec(ky.shape, lambda i, me: (0, 0, 0)),
    ]
    operands = [*arrived, maps, kz, ky]
    if acc is not None:
        in_specs.append(pl.BlockSpec(acc.shape, lambda i, me: (0, 0, 0)))
        operands.append(acc)
    image_shape = (2, kz_count, ky_count)
    outs = [jax.ShapeDtypeStruct(image_shape, jnp.float32)]
    if last and halves == 2:
        half_shape = (2, kz_count, ky_count // 2)
        outs = [jax.ShapeDtypeStruct(half_shape, jnp.float32), jax.ShapeDtypeStruct(half_shape, jnp.bfloat16)]
    return pl.pallas_call(
        functools.partial(image_kernel, acc is None, last, halves, lines, group, len(arrived)),
        out_shape=outs,
        grid_spec=pltpu.PrefetchScalarGridSpec(
            num_scalar_prefetch=1,
            grid=(coils // group,),
            in_specs=in_specs,
            out_specs=[pl.BlockSpec(o.shape, lambda i, me: (0, 0, 0)) for o in outs],
            scratch_shapes=[
                pltpu.VMEM(wide, jnp.float32),
                pltpu.VMEM((group, depth, packed), jnp.bfloat16),
                pltpu.VMEM((group, kz_count, 2 * depth), jnp.bfloat16),
                pltpu.VMEM(image_shape, jnp.float32),
            ],
        ),
        compiler_params=pltpu.CompilerParams(vmem_limit_bytes=VMEM_BYTES),
        name="image_of_coils",
    )(me, *operands)


def ranks(taken):
    lines = taken.shape[-1]
    before = jnp.asarray(np.triu(np.ones((lines, lines), np.float32), 1).astype(ml_dtypes.bfloat16))
    flat = taken.reshape(-1, lines).astype(jnp.bfloat16)
    rank = jnp.dot(flat, before, preferred_element_type=jnp.float32)
    return jnp.where(flat > 0, rank, -1.0).reshape(taken.shape)


def on_device(kspace, sensitivity, sampled, pole_y, order_y, pole_z, order_z):
    _, coils, readouts, lines, kz_count = kspace.shape
    devices = lax.axis_size("ro")
    halves = lax.axis_size("coil")
    ky_count = lines * devices
    stride = round_up(lines, 16)
    inner = 16 // math.gcd(lines, 16)
    outer = devices // inner
    parts = [(coils,), ()] if inner != 4 or coils != sum(FIRST + LATER) else [FIRST, LATER]
    planned = len(parts[1]) > 0
    place = lax.axis_index("ro")
    me = jnp.stack([lax.axis_index("coil"), place, place // inner, place % inner]).astype(jnp.int32)
    lines_first = jnp.swapaxes(kspace, 2, 3)
    maps = jnp.swapaxes(sensitivity, 3, 4)
    params = (sampled, pole_y, order_y, pole_z, order_z)
    kz = kz_table(kz_count)
    tables = ky_tables(ky_count, round_up(ky_count, LANES))
    ky = jnp.pad(tables.reshape(2, devices, lines, -1), ((0, 0), (0, 0), (0, stride - lines), (0, 0))).reshape(
        2, devices * stride, -1
    )

    def window(planes, start, count):
        return window_chunk(lines_first, me, params, inner, planes, start, count)

    def image(arrived, rows, by_line, start, count, acc, last=False):
        return image_chunk(
            arrived, maps, kz, rows, acc, me, inner, lines if by_line else 0, start, count, last, halves
        )

    def to_place(array, k):
        return lax.ppermute(array, "ro", [(a, a ^ k) for a in range(devices)])

    def in_plane(own, first, others):
        across = to_place(others, 2)
        return [own, to_place(first, 1), across, to_place(across[1], 1)]

    def to_planes(packed):
        same_place = [[p * inner + i for p in range(outer)] for i in range(inner)]
        return lax.all_to_all(
            packed, "ro", split_axis=0, concat_axis=0, tiled=True, axis_index_groups=same_place
        )

    def finish(result):
        if halves == 2:
            keep, give = result
            whole = keep + lax.ppermute(give, "coil", [(0, 1), (1, 0)]).astype(jnp.float32)
        else:
            whole = lax.psum_scatter(result[0], "coil", scatter_dimension=2, tiled=True)
        return jnp.swapaxes(whole, 1, 2)[:, None]

    def straight(first, plan):
        starts = [sum(plan[:i]) for i in range(len(plan))]
        acc, arrived = None, []
        for i, start in enumerate(starts):
            sent = first if i == 0 else window(0, start, plan[i])[0]
            if i >= 2:
                acc = image([arrived[i - 2]], ky, True, starts[i - 2], plan[i - 2], acc)[0]
                sent, acc = lax.optimization_barrier((sent, acc))
            arrived.append(lax.all_to_all(sent, "ro", split_axis=0, concat_axis=0, tiled=True))
        for i in range(max(len(plan) - 2, 0), len(plan)):
            result = image([arrived[i]], ky, True, starts[i], plan[i], acc, i == len(plan) - 1)
            acc = result[0]
        return finish(result)

    if not planned:
        return straight(window(0, 0, coils)[0], (coils,))

    starts = [sum((FIRST + LATER)[:i]) for i in range(len(FIRST + LATER))]
    first_starts, later_starts = starts[: len(FIRST)], starts[len(FIRST) :]

    def pack(held, slots):
        return pack_lines(held, slots, me, outer, inner, lines, SLOTS)

    def spread(part):
        return in_plane(*unpack_lines(part, sampled, me, inner, lines))

    def by_planes(one):
        plane_slots = ranks(sampled.reshape(readouts, outer, inner * lines))
        for_plane = plane_slots.reshape(readouts, devices, 1, lines)
        rows = pick_rows(tables, plane_slots[:, :, None], me, SLOTS, round_up(outer * SLOTS, LANES))
        second = window(0, first_starts[1], FIRST[1])
        later = [window(outer, start, count) for start, count in zip(later_starts, LATER)]
        one = to_planes(one)
        two, one, later[0] = lax.optimization_barrier((pack(second, sampled), one, later[0]))
        two = to_planes(two)
        gathered = [in_plane(*part) for part in later]
        acc = image(spread(one), ky, True, first_starts[0], FIRST[0], None)[0]
        here, acc, rows = lax.optimization_barrier((for_plane, acc, rows))
        three, two = lax.optimization_barrier((pack(gathered[0], here), two))
        three = to_planes(three)
        two = spread(two)
        four, acc, two, three = lax.optimization_barrier((pack(gathered[1], for_plane), acc, two, three))
        four = to_planes(four)
        acc = image(two, ky, True, first_starts[1], FIRST[1], acc)[0]
        acc = image([three], rows, False, later_starts[0], LATER[0], acc)[0]
        return finish(image([four], rows, False, later_starts[1], LATER[1], acc, True))

    first = window(0, 0, FIRST[0])[0]
    return lax.cond(
        most_lines(sampled, inner, outer) <= SLOTS,
        lambda first, packed: by_planes(packed),
        lambda first, packed: straight(first, STRAIGHT),
        first,
        pack([first], sampled),
    )


def solution(mesh):
    return jax.shard_map(
        on_device,
        mesh=mesh,
        in_specs=(
            P(None, "coil", None, "ro", None),
            P(None, "coil", "ro", None, None),
            P(),
            P(),
            P(),
            P(),
            P(),
        ),
        out_specs=P(None, "ro", "coil", None),
        check_vma=False,
    )
```

```python
import functools
import math

import jax
import jax.numpy as jnp
import ml_dtypes
import numpy as np
from jax import lax
from jax.experimental import pallas as pl
from jax.experimental.pallas import tpu as pltpu
from jax.sharding import PartitionSpec as P

LANES = 128
VMEM_BYTES = 56 * 2**20
FIRST, LATER = (4, 12), (12, 4)
STRAIGHT = (4, 24, 4)
SLOTS = 96


def round_up(value, step):
    return (value + step - 1) // step * step


def dft_tables(length):
    index = np.arange(length, dtype=np.int64)
    product = index[:, None] * index[None, :] % length
    angle = product.astype(np.float32) * np.float32(2.0 * math.pi / length)
    factor = np.float32(1.0 / math.sqrt(length))
    return (
        (np.cos(angle) * factor).astype(ml_dtypes.bfloat16).astype(np.float32),
        (np.sin(angle) * factor).astype(ml_dtypes.bfloat16).astype(np.float32),
    )


def kz_table(length):
    cosine, sine = dft_tables(length)
    table = np.block([[cosine, -sine], [sine, cosine]])
    return jnp.asarray(table.astype(ml_dtypes.bfloat16))


def ky_tables(length, width):
    def padded(part):
        table = np.zeros((length, width), np.float32)
        table[:, :length] = part.T
        return table

    cosine, sine = (padded(part) for part in dft_tables(length))
    table = np.stack([np.concatenate([cosine, sine], axis=1), np.concatenate([-sine, cosine], axis=1)])
    return jnp.asarray(table.astype(ml_dtypes.bfloat16))


def growth(quotient, order):
    square = quotient * quotient
    fourth = square * square
    return 1.0 + jnp.where(order < 1.5, square, jnp.where(order < 2.5, fourth, fourth * square))


def fold(index, length):
    return jnp.minimum(index, length - index).astype(jnp.float32)


def fill_weights(first, sampled_ref, pole_y_ref, order_y_ref, pole_z_ref, order_z_ref, weight):
    lines, readouts, kz_count = weight.shape
    ky_count = sampled_ref.shape[-1]
    width = round_up(lines, LANES)
    line = lax.broadcasted_iota(jnp.int32, (ky_count, width), 1) + first
    place = lax.broadcasted_iota(jnp.int32, (ky_count, width), 0)
    pick = (line == place).astype(jnp.bfloat16)

    def mine(ref):
        return jnp.dot(
            ref[...].astype(jnp.float32).astype(jnp.bfloat16), pick, preferred_element_type=jnp.float32
        )

    sampled, pole_z, order_z = mine(sampled_ref), mine(pole_z_ref), mine(order_z_ref)
    per_y = 1.0 / pole_y_ref[...].astype(jnp.float32)
    per_z = 1.0 / pole_z
    order_y = order_y_ref[...].astype(jnp.float32)
    freq_z = fold(lax.broadcasted_iota(jnp.int32, (readouts, kz_count), 1), kz_count)
    for k in range(lines):
        freq_y = fold(jnp.full((readouts, kz_count), first + k, jnp.int32), ky_count)
        column_y = growth(freq_y * per_y, order_y)
        column_z = growth(freq_z * per_z[:, k : k + 1], order_z[:, k : k + 1])
        weight[k] = sampled[:, k : k + 1] / (column_y * column_z)


def fill_lines(x_ref, weight, packed, coils):
    _, _, lines, readouts, _ = x_ref.shape

    def one(k, _):
        w = weight[k]
        for n, c in enumerate(coils):
            at = pl.ds(pl.multiple_of((n * lines + k) * readouts, 16), readouts)
            line = jnp.concatenate([x_ref[part, c, k].astype(jnp.float32) * w for part in range(2)], axis=1)
            for t in range(packed.shape[0]):
                packed[t, at, :] = line[:, t * LANES : (t + 1) * LANES]
        return 0

    lax.fori_loop(0, lines, one, 0, unroll=4 if lines % 4 == 0 else 2)


def window_kernel(planes, me_ref, x_ref, *refs):
    params, refs = refs[:5], refs[5:]
    outs, (weight, packed) = refs[:-2], refs[-2:]
    _, group, lines, readouts, _ = x_ref.shape

    @pl.when(pl.program_id(0) == 0)
    def _():
        fill_weights(me_ref[1] * lines, *params, weight)

    fill_lines(x_ref, weight, packed, range(group))
    for r in range(readouts):
        k = r % 4 if planes else 0
        readout = r - k + (me_ref[3] ^ k) if planes else r
        o_ref = outs[0].at[r]
        if planes:
            o_ref = outs[k].at[r // 4] if k < 2 else outs[2].at[k - 2, r // 4]
        for t in range(packed.shape[0]):
            o_ref[:, t * LANES : (t + 1) * LANES] = packed[
                t, pl.ds(readout, group * lines, stride=readouts), :
            ].astype(jnp.bfloat16)


def window_chunk(lines_first, me, params, group, planes, start, coils):
    _, _, lines, readouts, kz_count = lines_first.shape
    rows = group * lines
    tail = (coils * lines, 2 * kz_count)
    whole = [pl.BlockSpec(p.shape, lambda i, me: (0, 0)) for p in params]
    heads = [(planes,), (planes,), (2, planes)] if planes else [(readouts,)]
    return pl.pallas_call(
        functools.partial(window_kernel, planes),
        out_shape=[jax.ShapeDtypeStruct((*h, *tail), jnp.bfloat16) for h in heads],
        grid_spec=pltpu.PrefetchScalarGridSpec(
            num_scalar_prefetch=1,
            grid=(coils // group,),
            in_specs=[
                pl.BlockSpec(
                    (2, group, lines, readouts, kz_count), lambda i, me: (0, i + start // group, 0, 0, 0)
                ),
                *whole,
            ],
            out_specs=[
                pl.BlockSpec((*h, rows, tail[1]), lambda i, me, h=h: (*(0 for _ in h), i, 0)) for h in heads
            ],
            scratch_shapes=[
                pltpu.VMEM((lines, readouts, kz_count), jnp.float32),
                pltpu.VMEM((2 * kz_count // LANES, rows * readouts, LANES), jnp.float32),
            ],
        ),
        compiler_params=pltpu.CompilerParams(vmem_limit_bytes=VMEM_BYTES),
        name="window_lines",
    )(me, lines_first, *params)


def one_hot(slots, count):
    row = lax.broadcasted_iota(jnp.int32, (count, slots.shape[-1]), 0).astype(jnp.float32)
    return (row == slots).astype(jnp.bfloat16)


def taken_lines(sampled_ref, first, lines):
    ky_count = sampled_ref.shape[-1]
    place = lax.broadcasted_iota(jnp.int32, (ky_count, LANES), 0)
    lane = lax.broadcasted_iota(jnp.int32, (ky_count, LANES), 1)
    pick = jnp.logical_and(lane + first == place, lane < lines).astype(jnp.bfloat16)
    return jnp.dot(
        sampled_ref[...].astype(jnp.float32).astype(jnp.bfloat16), pick, preferred_element_type=jnp.float32
    )


def source_slots(sampled_ref, source, lines, inner):
    taken = taken_lines(sampled_ref, source * lines, lines)
    readouts = taken.shape[0]
    row = lax.broadcasted_iota(jnp.int32, (LANES, LANES), 0)
    before = (row < lax.broadcasted_iota(jnp.int32, (LANES, LANES), 1)).astype(jnp.bfloat16)
    rank = jnp.dot(taken.astype(jnp.bfloat16), before, preferred_element_type=jnp.float32)
    owner = lax.broadcasted_iota(jnp.int32, (readouts, readouts), 0)
    other = lax.broadcasted_iota(jnp.int32, (readouts, readouts), 1)
    ahead = jnp.logical_and(owner // inner == other // inner, other < owner).astype(jnp.bfloat16)
    past = jnp.dot(ahead, taken.astype(jnp.bfloat16), preferred_element_type=jnp.float32)
    return jnp.where(taken > 0, rank + jnp.sum(past, axis=1, keepdims=True), -1.0)


def among(slots, c, group):
    empty = jnp.full_like(slots, -1.0)
    return [slots if n == c else empty for n in range(group)]


def pack_kernel(by_owner, me_ref, slots_ref, *refs):
    xs, (o_ref, picks) = refs[:-2], refs[-2:]
    outer, group, count, _ = o_ref.shape
    place, plane, within = me_ref[1], me_ref[2], me_ref[3]
    inner, rows = (xs[0].shape[0] // outer, xs[0].shape[1]) if by_owner else (len(xs), xs[0].shape[1])
    lines = rows // group

    @pl.when(pl.program_id(0) == 0)
    def _():
        if by_owner:
            own = source_slots(slots_ref, place, lines, inner)
        for p in range(outer):
            if by_owner:
                slots = [own[p * inner + k : p * inner + k + 1, :lines] for k in range(inner)]
            else:
                slots = [slots_ref[p * inner + within, plane * inner + (within ^ k)] for k in range(inner)]
            for c in range(group):
                picks[p, c] = one_hot(jnp.concatenate(sum([among(s, c, group) for s in slots], []), axis=1), count)

    for p in range(outer):
        blocks = [xs[0][p * inner + k] for k in range(inner)] if by_owner else [x[p] for x in xs]
        held = jnp.concatenate(blocks, axis=0)
        for c in range(group):
            o_ref[p, c] = jnp.dot(picks[p, c], held, preferred_element_type=jnp.float32).astype(jnp.bfloat16)


def block_specs(arrays, rows):
    return [
        pl.BlockSpec((x.shape[0], rows, x.shape[2]), lambda i, me: (0, i, 0))
        if x.ndim == 3
        else pl.BlockSpec((None, x.shape[1], rows, x.shape[3]), lambda i, me: (0, 0, i, 0))
        for x in arrays
    ]


def pack_lines(held, slots, me, outer, inner, lines, count):
    rows_all, packed = held[0].shape[-2:]
    group = inner
    rows = group * lines
    coils = rows_all // lines
    return pl.pallas_call(
        functools.partial(pack_kernel, len(held) == 1),
        out_shape=jax.ShapeDtypeStruct((outer, coils, count, packed), jnp.bfloat16),
        grid_spec=pltpu.PrefetchScalarGridSpec(
            num_scalar_prefetch=1,
            grid=(coils // group,),
            in_specs=[pl.BlockSpec(slots.shape, lambda i, me: (0,) * slots.ndim), *block_specs(held, rows)],
            out_specs=pl.BlockSpec((outer, group, count, packed), lambda i, me: (0, i, 0, 0)),
            scratch_shapes=[pltpu.VMEM((outer, group, count, inner * rows), jnp.bfloat16)],
        ),
        compiler_params=pltpu.CompilerParams(vmem_limit_bytes=VMEM_BYTES),
        name="pack_sampled",
    )(me, slots, *held)


def unpack_kernel(me_ref, sampled_ref, x_ref, own_ref, first_ref, others_ref, places, ranks):
    outer, group, count, packed = x_ref.shape
    inner, rows = places.shape[1], places.shape[2]
    lines = rows // group
    plane, within = me_ref[2], me_ref[3]

    @pl.when(pl.program_id(0) == 0)
    def _():
        for p in range(outer):
            ranks[...] = source_slots(sampled_ref, p * inner + within, lines, inner)
            for k in range(inner):
                slots = ranks[pl.ds(plane * inner + (within ^ k), 1), :][:, :lines]
                row = [jnp.where(slots >= 0, slots + c * count, -1.0) for c in range(group)]
                row = jnp.concatenate([*row, jnp.full((1, -rows % LANES), -1.0, jnp.float32)], axis=1)
                spread = one_hot(row, group * count).astype(jnp.float32).T
                places[p, k] = spread[:rows].astype(jnp.bfloat16)

    for p in range(outer):
        held = x_ref[p].reshape(group * count, packed)
        for k in range(inner):
            out = own_ref.at[p] if k == 0 else first_ref.at[p] if k == 1 else others_ref.at[k - 2, p]
            out[...] = jnp.dot(places[p, k], held, preferred_element_type=jnp.float32).astype(jnp.bfloat16)


def unpack_lines(arrived, sampled, me, inner, lines):
    outer, coils, count, packed = arrived.shape
    group = inner
    rows = group * lines
    tail = (coils * lines, packed)
    heads = [(outer,), (outer,), (2, outer)]
    return pl.pallas_call(
        unpack_kernel,
        out_shape=[jax.ShapeDtypeStruct((*h, *tail), jnp.bfloat16) for h in heads],
        grid_spec=pltpu.PrefetchScalarGridSpec(
            num_scalar_prefetch=1,
            grid=(coils // group,),
            in_specs=[
                pl.BlockSpec(sampled.shape, lambda i, me: (0, 0)),
                pl.BlockSpec((outer, group, count, packed), lambda i, me: (0, i, 0, 0)),
            ],
            out_specs=[
                pl.BlockSpec((*h, rows, packed), lambda i, me, h=h: (*(0 for _ in h), i, 0)) for h in heads
            ],
            scratch_shapes=[
                pltpu.VMEM((outer, inner, rows, group * count), jnp.bfloat16),
                pltpu.VMEM((sampled.shape[0], LANES), jnp.float32),
            ],
        ),
        compiler_params=pltpu.CompilerParams(vmem_limit_bytes=VMEM_BYTES),
        name="unpack_sampled",
    )(me, sampled, arrived)


def most_kernel(inner, outer, sampled_ref, o_ref):
    readouts, ky_count = sampled_ref.shape
    devices = inner * outer
    taken = sampled_ref[...].astype(jnp.float32).astype(jnp.bfloat16)
    line = lax.broadcasted_iota(jnp.int32, (ky_count, LANES), 0)
    lane = lax.broadcasted_iota(jnp.int32, (ky_count, LANES), 1)

    def sums(parts):
        return jnp.dot(
            taken, (line // (ky_count // parts) == lane).astype(jnp.bfloat16), preferred_element_type=jnp.float32
        )

    row = lax.broadcasted_iota(jnp.int32, (readouts, readouts), 0)
    readout = lax.broadcasted_iota(jnp.int32, (readouts, readouts), 1)
    together = (row // inner == readout // inner).astype(jnp.bfloat16)
    by_source = jnp.dot(together, sums(devices).astype(jnp.bfloat16), preferred_element_type=jnp.float32)
    o_ref[0, 0] = jnp.max(jnp.maximum(by_source, sums(outer))).astype(jnp.int32)


def first_kernel(inner, outer, me_ref, x_ref, *refs):
    params, (o_ref, packed_ref, most_ref, weight, tiles, picks) = refs[:5], refs[5:]
    window_kernel(0, me_ref, x_ref, *params, o_ref, weight, tiles)
    pack_kernel(True, me_ref, params[0], o_ref, packed_ref, picks)
    most_kernel(inner, outer, params[0], most_ref)


def first_chunk(lines_first, me, params, inner, outer, count):
    _, _, lines, readouts, kz_count = lines_first.shape
    rows, packed = inner * lines, 2 * kz_count
    shapes = [(readouts, rows, packed), (outer, inner, count, packed)]
    whole = [pl.BlockSpec(p.shape, lambda i, me: (0, 0)) for p in params]
    *arrays, most = pl.pallas_call(
        functools.partial(first_kernel, inner, outer),
        out_shape=[*(jax.ShapeDtypeStruct(s, jnp.bfloat16) for s in shapes), jax.ShapeDtypeStruct((1, 1), jnp.int32)],
        grid_spec=pltpu.PrefetchScalarGridSpec(
            num_scalar_prefetch=1,
            grid=(1,),
            in_specs=[pl.BlockSpec((2, inner, lines, readouts, kz_count), lambda i, me: (0, 0, 0, 0, 0)), *whole],
            out_specs=[
                *(pl.BlockSpec(s, lambda i, me, n=len(s): (0,) * n) for s in shapes),
                pl.BlockSpec(memory_space=pltpu.SMEM),
            ],
            scratch_shapes=[
                pltpu.VMEM((lines, readouts, kz_count), jnp.float32),
                pltpu.VMEM((packed // LANES, rows * readouts, LANES), jnp.float32),
                pltpu.VMEM((outer, inner, count, inner * rows), jnp.bfloat16),
            ],
        ),
        compiler_params=pltpu.CompilerParams(vmem_limit_bytes=VMEM_BYTES),
        name="window_and_pack",
    )(me, lines_first, *params)
    return *arrays, most[0, 0]


def pick_kernel(count, me_ref, slots_ref, table_ref, o_ref):
    o_ref[...] = jnp.zeros_like(o_ref)
    for p in range(slots_ref.shape[1]):
        pick = one_hot(slots_ref[me_ref[1], p], count)
        for part in range(2):
            o_ref[part, pl.ds(p * count, count), :] = jnp.dot(
                pick, table_ref[part, p], preferred_element_type=jnp.float32
            ).astype(jnp.bfloat16)


def pick_rows(table, slots, me, count, depth):
    outer = slots.shape[1]
    table = table.reshape(2, outer, table.shape[1] // outer, table.shape[2])
    shape = (2, depth, table.shape[3])
    return pl.pallas_call(
        functools.partial(pick_kernel, count),
        out_shape=jax.ShapeDtypeStruct(shape, jnp.bfloat16),
        grid_spec=pltpu.PrefetchScalarGridSpec(
            num_scalar_prefetch=1,
            grid=(1,),
            in_specs=[
                pl.BlockSpec(slots.shape, lambda i, me: (0, 0, 0, 0)),
                pl.BlockSpec(table.shape, lambda i, me: (0, 0, 0, 0)),
            ],
            out_specs=pl.BlockSpec(shape, lambda i, me: (0, 0, 0)),
        ),
        compiler_params=pltpu.CompilerParams(vmem_limit_bytes=VMEM_BYTES),
        name="pick_table_rows",
    )(me, slots, table)


def image_kernel(fresh, last, halves, lines, group, pieces, me_ref, *refs):
    xs, refs = refs[:pieces], list(refs[pieces:])
    x_ref, (maps_ref, kz_ref, ky_ref), refs = xs[0], refs[:3], refs[3:]
    acc_in = None if fresh else refs.pop(0)
    outs, (wide, by_line, hybrid, acc) = refs[:-4], refs[-4:]
    kz_count, ky_count = maps_ref.shape[-2:]
    depth = by_line.shape[1]
    width = ky_ref.shape[-1] // 2
    step = pl.program_id(0)

    @pl.when(step == 0)
    def _():
        acc[...] = jnp.zeros_like(acc) if fresh else acc_in[...]
        by_line[...] = jnp.zeros_like(by_line)

    if lines:
        stride = depth // (x_ref.shape[0] * pieces)

        for k in range(pieces):

            def place(s, _, k=k):
                wide[k % 2] = xs[k][s].astype(jnp.float32)
                source = s * pieces + (me_ref[3] ^ k) if pieces > 1 else s
                base = pl.multiple_of(source * stride, stride)
                for c in range(group):
                    by_line[c, pl.ds(base, lines), :] = wide[k % 2, pl.ds(lines * c, lines), :].astype(jnp.bfloat16)
                return 0

            lax.fori_loop(0, x_ref.shape[0], place, 0)
    else:
        count = x_ref.shape[2]
        for c in range(group):
            for p in range(x_ref.shape[0]):
                by_line[c, p * count : (p + 1) * count, :] = x_ref[p, c]

    for c in range(group):
        mixed = lax.dot_general(
            kz_ref[...], by_line[c], (((1,), (1,)), ((), ())), preferred_element_type=jnp.float32
        )
        hybrid[c, :, :depth] = mixed[:kz_count].astype(jnp.bfloat16)
        hybrid[c, :, depth:] = mixed[kz_count:].astype(jnp.bfloat16)
    for c in range(group):
        image = jnp.dot(
            hybrid[c], ky_ref[...].reshape(2 * depth, 2 * width), preferred_element_type=jnp.float32
        )
        real, imag = image[:, :ky_count], image[:, width : width + ky_count]
        map_real = maps_ref[0, c, 0].astype(jnp.float32)
        map_imag = maps_ref[1, c, 0].astype(jnp.float32)
        acc[0] += map_real * real + map_imag * imag
        acc[1] += map_real * imag - map_imag * real

    @pl.when(step == pl.num_programs(0) - 1)
    def _():
        if last and halves == 2:
            keep_ref, send_ref = outs
            rows = ky_count // 2
            lower = me_ref[0] == 0
            for part in range(2):
                low, high = acc[part, :, :rows], acc[part, :, rows:]
                keep_ref[part] = jnp.where(lower, low, high)
                send_ref[part] = jnp.where(lower, high, low).astype(send_ref.dtype)
        else:
            outs[0][...] = acc[...]


def image_chunk(arrived, maps, kz, ky, acc, me, group, lines, start, coils, last, halves):
    kz_count, ky_count = maps.shape[-2:]
    packed = arrived[0].shape[-1]
    depth = ky.shape[1]
    if lines:
        x_specs = block_specs(arrived, group * lines)
    else:
        group = 2 if last else group
        x_specs = [
            pl.BlockSpec((x.shape[0], group, *x.shape[2:]), lambda i, me: (0, i, 0, 0)) for x in arrived
        ]
    wide = (2, max(group * lines, 8), packed)
    in_specs = [
        *x_specs,
        pl.BlockSpec((2, group, 1, kz_count, ky_count), lambda i, me: (0, i + start // group, 0, 0, 0)),
        pl.BlockSpec(kz.shape, lambda i, me: (0, 0)),
        pl.BlockSpec(ky.shape, lambda i, me: (0, 0, 0)),
    ]
    operands = [*arrived, maps, kz, ky]
    if acc is not None:
        in_specs.append(pl.BlockSpec(acc.shape, lambda i, me: (0, 0, 0)))
        operands.append(acc)
    image_shape = (2, kz_count, ky_count)
    outs = [jax.ShapeDtypeStruct(image_shape, jnp.float32)]
    if last and halves == 2:
        half_shape = (2, kz_count, ky_count // 2)
        outs = [jax.ShapeDtypeStruct(half_shape, jnp.float32), jax.ShapeDtypeStruct(half_shape, jnp.bfloat16)]
    return pl.pallas_call(
        functools.partial(image_kernel, acc is None, last, halves, lines, group, len(arrived)),
        out_shape=outs,
        grid_spec=pltpu.PrefetchScalarGridSpec(
            num_scalar_prefetch=1,
            grid=(coils // group,),
            in_specs=in_specs,
            out_specs=[pl.BlockSpec(o.shape, lambda i, me: (0, 0, 0)) for o in outs],
            scratch_shapes=[
                pltpu.VMEM(wide, jnp.float32),
                pltpu.VMEM((group, depth, packed), jnp.bfloat16),
                pltpu.VMEM((group, kz_count, 2 * depth), jnp.bfloat16),
                pltpu.VMEM(image_shape, jnp.float32),
            ],
        ),
        compiler_params=pltpu.CompilerParams(vmem_limit_bytes=VMEM_BYTES),
        name="image_of_coils",
    )(me, *operands)


def ranks(taken):
    lines = taken.shape[-1]
    before = jnp.asarray(np.triu(np.ones((lines, lines), np.float32), 1).astype(ml_dtypes.bfloat16))
    flat = taken.reshape(-1, lines).astype(jnp.bfloat16)
    rank = jnp.dot(flat, before, preferred_element_type=jnp.float32)
    return jnp.where(flat > 0, rank, -1.0).reshape(taken.shape)


def on_device(kspace, sensitivity, sampled, pole_y, order_y, pole_z, order_z):
    _, coils, readouts, lines, kz_count = kspace.shape
    devices = lax.axis_size("ro")
    halves = lax.axis_size("coil")
    ky_count = lines * devices
    stride = round_up(lines, 16)
    inner = 16 // math.gcd(lines, 16)
    outer = devices // inner
    parts = [(coils,), ()] if inner != 4 or coils != sum(FIRST + LATER) else [FIRST, LATER]
    planned = len(parts[1]) > 0 and FIRST[0] == STRAIGHT[0] == inner
    place = lax.axis_index("ro")
    me = jnp.stack([lax.axis_index("coil"), place, place // inner, place % inner]).astype(jnp.int32)
    lines_first = jnp.swapaxes(kspace, 2, 3)
    maps = jnp.swapaxes(sensitivity, 3, 4)
    params = (sampled, pole_y, order_y, pole_z, order_z)
    kz = kz_table(kz_count)
    tables = ky_tables(ky_count, round_up(ky_count, LANES))
    ky = jnp.pad(tables.reshape(2, devices, lines, -1), ((0, 0), (0, 0), (0, stride - lines), (0, 0))).reshape(
        2, devices * stride, -1
    )

    def window(planes, start, count):
        return window_chunk(lines_first, me, params, inner, planes, start, count)

    def image(arrived, rows, by_line, start, count, acc, last=False):
        return image_chunk(
            arrived, maps, kz, rows, acc, me, inner, lines if by_line else 0, start, count, last, halves
        )

    def to_place(array, k):
        return lax.ppermute(array, "ro", [(a, a ^ k) for a in range(devices)])

    def in_plane(own, first, others):
        across = to_place(others, 2)
        return [own, to_place(first, 1), across, to_place(across[1], 1)]

    def to_planes(packed):
        same_place = [[p * inner + i for p in range(outer)] for i in range(inner)]
        return lax.all_to_all(
            packed, "ro", split_axis=0, concat_axis=0, tiled=True, axis_index_groups=same_place
        )

    def finish(result):
        if halves == 2:
            keep, give = result
            whole = keep + lax.ppermute(give, "coil", [(0, 1), (1, 0)]).astype(jnp.float32)
        else:
            whole = lax.psum_scatter(result[0], "coil", scatter_dimension=2, tiled=True)
        return jnp.swapaxes(whole, 1, 2)[:, None]

    def straight(first, plan):
        starts = [sum(plan[:i]) for i in range(len(plan))]
        acc, arrived = None, []
        for i, start in enumerate(starts):
            sent = first if i == 0 else window(0, start, plan[i])[0]
            if i >= 2:
                acc = image([arrived[i - 2]], ky, True, starts[i - 2], plan[i - 2], acc)[0]
                sent, acc = lax.optimization_barrier((sent, acc))
            arrived.append(lax.all_to_all(sent, "ro", split_axis=0, concat_axis=0, tiled=True))
        for i in range(max(len(plan) - 2, 0), len(plan)):
            result = image([arrived[i]], ky, True, starts[i], plan[i], acc, i == len(plan) - 1)
            acc = result[0]
        return finish(result)

    if not planned:
        return straight(window(0, 0, coils)[0], (coils,))

    starts = [sum((FIRST + LATER)[:i]) for i in range(len(FIRST + LATER))]
    first_starts, later_starts = starts[: len(FIRST)], starts[len(FIRST) :]

    def pack(held, slots):
        return pack_lines(held, slots, me, outer, inner, lines, SLOTS)

    def spread(part):
        return in_plane(*unpack_lines(part, sampled, me, inner, lines))

    def by_planes(one):
        plane_slots = ranks(sampled.reshape(readouts, outer, inner * lines))
        for_plane = plane_slots.reshape(readouts, devices, 1, lines)
        rows = pick_rows(tables, plane_slots[:, :, None], me, SLOTS, round_up(outer * SLOTS, LANES))
        second = window(0, first_starts[1], FIRST[1])
        third = window(outer, later_starts[0], LATER[0])
        one = to_planes(one)
        two, one, third = lax.optimization_barrier((pack(second, sampled), one, third))
        two = to_planes(two)
        third = in_plane(*third)
        one = spread(one)
        here, one, rows = lax.optimization_barrier((for_plane, one, rows))
        three, two = lax.optimization_barrier((pack(third, here), two))
        three = to_planes(three)
        acc = image(one, ky, True, first_starts[0], FIRST[0], None)[0]
        after, acc = lax.optimization_barrier((me, acc))
        two = spread(two)
        fourth = in_plane(*window_chunk(lines_first, after, params, inner, outer, later_starts[1], LATER[1]))
        four, acc, two, three = lax.optimization_barrier((pack(fourth, for_plane), acc, two, three))
        four = to_planes(four)
        acc = image(two, ky, True, first_starts[1], FIRST[1], acc)[0]
        acc = image([three], rows, False, later_starts[0], LATER[0], acc)[0]
        return finish(image([four], rows, False, later_starts[1], LATER[1], acc, True))

    first, packed, most = first_chunk(lines_first, me, params, inner, outer, SLOTS)
    return lax.cond(
        most <= SLOTS,
        lambda first, packed: by_planes(packed),
        lambda first, packed: straight(first, STRAIGHT),
        first,
        packed,
    )


def solution(mesh):
    return jax.shard_map(
        on_device,
        mesh=mesh,
        in_specs=(
            P(None, "coil", None, "ro", None),
            P(None, "coil", "ro", None, None),
            P(),
            P(),
            P(),
            P(),
            P(),
        ),
        out_specs=P(None, "ro", "coil", None),
        check_vma=False,
    )
```

```python
import functools
import math

import jax
import jax.numpy as jnp
import ml_dtypes
import numpy as np
from jax import lax
from jax.experimental import pallas as pl
from jax.experimental.pallas import tpu as pltpu
from jax.sharding import PartitionSpec as P

LANES = 128
BUFFERS = 4
VMEM_BYTES = 56 * 2**20
FIRST, LATER = (4, 12), (12, 4)
STRAIGHT = (4, 24, 4)
SLOTS = 96


def round_up(value, step):
    return (value + step - 1) // step * step


def dft_tables(length):
    index = np.arange(length, dtype=np.int64)
    product = index[:, None] * index[None, :] % length
    angle = product.astype(np.float32) * np.float32(2.0 * math.pi / length)
    factor = np.float32(1.0 / math.sqrt(length))
    return (
        (np.cos(angle) * factor).astype(ml_dtypes.bfloat16).astype(np.float32),
        (np.sin(angle) * factor).astype(ml_dtypes.bfloat16).astype(np.float32),
    )


def kz_table(length):
    cosine, sine = dft_tables(length)
    table = np.block([[cosine, -sine], [sine, cosine]])
    return jnp.asarray(table.astype(ml_dtypes.bfloat16))


def ky_tables(length, width):
    def padded(part):
        table = np.zeros((length, width), np.float32)
        table[:, :length] = part.T
        return table

    cosine, sine = (padded(part) for part in dft_tables(length))
    table = np.stack([np.concatenate([cosine, sine], axis=1), np.concatenate([-sine, cosine], axis=1)])
    return jnp.asarray(table.astype(ml_dtypes.bfloat16))


def growth(quotient, order):
    square = quotient * quotient
    fourth = square * square
    return 1.0 + jnp.where(order < 1.5, square, jnp.where(order < 2.5, fourth, fourth * square))


def fold(index, length):
    return jnp.minimum(index, length - index).astype(jnp.float32)


def fill_weights(first, sampled_ref, pole_y_ref, order_y_ref, pole_z_ref, order_z_ref, weight):
    lines, readouts, kz_count = weight.shape
    ky_count = sampled_ref.shape[-1]
    width = round_up(lines, LANES)
    line = lax.broadcasted_iota(jnp.int32, (ky_count, width), 1) + first
    place = lax.broadcasted_iota(jnp.int32, (ky_count, width), 0)
    pick = (line == place).astype(jnp.bfloat16)

    def mine(ref):
        return jnp.dot(
            ref[...].astype(jnp.float32).astype(jnp.bfloat16), pick, preferred_element_type=jnp.float32
        )

    sampled, pole_z, order_z = mine(sampled_ref), mine(pole_z_ref), mine(order_z_ref)
    per_y = 1.0 / pole_y_ref[...].astype(jnp.float32)
    per_z = 1.0 / pole_z
    order_y = order_y_ref[...].astype(jnp.float32)
    freq_z = fold(lax.broadcasted_iota(jnp.int32, (readouts, kz_count), 1), kz_count)
    for k in range(lines):
        freq_y = fold(jnp.full((readouts, kz_count), first + k, jnp.int32), ky_count)
        column_y = growth(freq_y * per_y, order_y)
        column_z = growth(freq_z * per_z[:, k : k + 1], order_z[:, k : k + 1])
        weight[k] = sampled[:, k : k + 1] / (column_y * column_z)


def fill_lines(x_ref, weight, packed, coils):
    _, _, lines, readouts, _ = x_ref.shape

    def one(k, _):
        w = weight[k]
        for n, c in enumerate(coils):
            at = pl.ds(pl.multiple_of((n * lines + k) * readouts, 16), readouts)
            line = jnp.concatenate([x_ref[part, c, k].astype(jnp.float32) * w for part in range(2)], axis=1)
            for t in range(packed.shape[0]):
                packed[t, at, :] = line[:, t * LANES : (t + 1) * LANES]
        return 0

    lax.fori_loop(0, lines, one, 0, unroll=4 if lines % 4 == 0 else 2)


def window_kernel(planes, me_ref, x_ref, *refs):
    params, refs = refs[:5], refs[5:]
    outs, (weight, packed) = refs[:-2], refs[-2:]
    _, group, lines, readouts, _ = x_ref.shape

    @pl.when(pl.program_id(0) == 0)
    def _():
        fill_weights(me_ref[1] * lines, *params, weight)

    fill_lines(x_ref, weight, packed, range(group))
    for r in range(readouts):
        k = r % 4 if planes else 0
        readout = r - k + (me_ref[3] ^ k) if planes else r
        o_ref = outs[0].at[r]
        if planes:
            o_ref = outs[k].at[r // 4] if k < 2 else outs[2].at[k - 2, r // 4]
        for t in range(packed.shape[0]):
            o_ref[:, t * LANES : (t + 1) * LANES] = packed[
                t, pl.ds(readout, group * lines, stride=readouts), :
            ].astype(jnp.bfloat16)


def window_chunk(lines_first, me, params, group, planes, start, coils):
    _, _, lines, readouts, kz_count = lines_first.shape
    rows = group * lines
    tail = (coils * lines, 2 * kz_count)
    whole = [pl.BlockSpec(p.shape, lambda i, me: (0, 0)) for p in params]
    heads = [(planes,), (planes,), (2, planes)] if planes else [(readouts,)]
    return pl.pallas_call(
        functools.partial(window_kernel, planes),
        out_shape=[jax.ShapeDtypeStruct((*h, *tail), jnp.bfloat16) for h in heads],
        grid_spec=pltpu.PrefetchScalarGridSpec(
            num_scalar_prefetch=1,
            grid=(coils // group,),
            in_specs=[
                pl.BlockSpec(
                    (2, group, lines, readouts, kz_count), lambda i, me: (0, i + start // group, 0, 0, 0)
                ),
                *whole,
            ],
            out_specs=[
                pl.BlockSpec((*h, rows, tail[1]), lambda i, me, h=h: (*(0 for _ in h), i, 0)) for h in heads
            ],
            scratch_shapes=[
                pltpu.VMEM((lines, readouts, kz_count), jnp.float32),
                pltpu.VMEM((2 * kz_count // LANES, rows * readouts, LANES), jnp.float32),
            ],
        ),
        compiler_params=pltpu.CompilerParams(vmem_limit_bytes=VMEM_BYTES),
        name="window_lines",
    )(me, lines_first, *params)


def one_hot(slots, count):
    row = lax.broadcasted_iota(jnp.int32, (count, slots.shape[-1]), 0).astype(jnp.float32)
    return (row == slots).astype(jnp.bfloat16)


def taken_lines(sampled_ref, first, lines):
    ky_count = sampled_ref.shape[-1]
    place = lax.broadcasted_iota(jnp.int32, (ky_count, LANES), 0)
    lane = lax.broadcasted_iota(jnp.int32, (ky_count, LANES), 1)
    pick = jnp.logical_and(lane + first == place, lane < lines).astype(jnp.bfloat16)
    return jnp.dot(
        sampled_ref[...].astype(jnp.float32).astype(jnp.bfloat16), pick, preferred_element_type=jnp.float32
    )


def source_slots(sampled_ref, source, lines, inner):
    taken = taken_lines(sampled_ref, source * lines, lines)
    readouts = taken.shape[0]
    row = lax.broadcasted_iota(jnp.int32, (LANES, LANES), 0)
    before = (row < lax.broadcasted_iota(jnp.int32, (LANES, LANES), 1)).astype(jnp.bfloat16)
    rank = jnp.dot(taken.astype(jnp.bfloat16), before, preferred_element_type=jnp.float32)
    owner = lax.broadcasted_iota(jnp.int32, (readouts, readouts), 0)
    other = lax.broadcasted_iota(jnp.int32, (readouts, readouts), 1)
    ahead = jnp.logical_and(owner // inner == other // inner, other < owner).astype(jnp.bfloat16)
    past = jnp.dot(ahead, taken.astype(jnp.bfloat16), preferred_element_type=jnp.float32)
    return jnp.where(taken > 0, rank + jnp.sum(past, axis=1, keepdims=True), -1.0)


def among(slots, c, group):
    empty = jnp.full_like(slots, -1.0)
    return [slots if n == c else empty for n in range(group)]


def pack_kernel(by_owner, me_ref, slots_ref, *refs):
    xs, (o_ref, picks) = refs[:-2], refs[-2:]
    outer, group, count, _ = o_ref.shape
    place, plane, within = me_ref[1], me_ref[2], me_ref[3]
    inner, rows = (xs[0].shape[0] // outer, xs[0].shape[1]) if by_owner else (len(xs), xs[0].shape[1])
    lines = rows // group

    @pl.when(pl.program_id(0) == 0)
    def _():
        if by_owner:
            own = source_slots(slots_ref, place, lines, inner)
        for p in range(outer):
            if by_owner:
                slots = [own[p * inner + k : p * inner + k + 1, :lines] for k in range(inner)]
            else:
                slots = [slots_ref[p * inner + within, plane * inner + (within ^ k)] for k in range(inner)]
            for c in range(group):
                picks[p, c] = one_hot(jnp.concatenate(sum([among(s, c, group) for s in slots], []), axis=1), count)

    for p in range(outer):
        blocks = [xs[0][p * inner + k] for k in range(inner)] if by_owner else [x[p] for x in xs]
        held = jnp.concatenate(blocks, axis=0)
        for c in range(group):
            o_ref[p, c] = jnp.dot(picks[p, c], held, preferred_element_type=jnp.float32).astype(jnp.bfloat16)


def block_specs(arrays, rows):
    return [
        pl.BlockSpec((x.shape[0], rows, x.shape[2]), lambda i, me: (0, i, 0))
        if x.ndim == 3
        else pl.BlockSpec((None, x.shape[1], rows, x.shape[3]), lambda i, me: (0, 0, i, 0))
        for x in arrays
    ]


def pack_lines(held, slots, me, outer, inner, lines, count):
    rows_all, packed = held[0].shape[-2:]
    group = inner
    rows = group * lines
    coils = rows_all // lines
    return pl.pallas_call(
        functools.partial(pack_kernel, len(held) == 1),
        out_shape=jax.ShapeDtypeStruct((outer, coils, count, packed), jnp.bfloat16),
        grid_spec=pltpu.PrefetchScalarGridSpec(
            num_scalar_prefetch=1,
            grid=(coils // group,),
            in_specs=[pl.BlockSpec(slots.shape, lambda i, me: (0,) * slots.ndim), *block_specs(held, rows)],
            out_specs=pl.BlockSpec((outer, group, count, packed), lambda i, me: (0, i, 0, 0)),
            scratch_shapes=[pltpu.VMEM((outer, group, count, inner * rows), jnp.bfloat16)],
        ),
        compiler_params=pltpu.CompilerParams(vmem_limit_bytes=VMEM_BYTES),
        name="pack_sampled",
    )(me, slots, *held)


def unpack_kernel(me_ref, sampled_ref, x_ref, own_ref, first_ref, others_ref, places, ranks):
    outer, group, count, packed = x_ref.shape
    inner, rows = places.shape[1], places.shape[2]
    lines = rows // group
    plane, within = me_ref[2], me_ref[3]

    @pl.when(pl.program_id(0) == 0)
    def _():
        for p in range(outer):
            ranks[...] = source_slots(sampled_ref, p * inner + within, lines, inner)
            for k in range(inner):
                slots = ranks[pl.ds(plane * inner + (within ^ k), 1), :][:, :lines]
                row = [jnp.where(slots >= 0, slots + c * count, -1.0) for c in range(group)]
                row = jnp.concatenate([*row, jnp.full((1, -rows % LANES), -1.0, jnp.float32)], axis=1)
                spread = one_hot(row, group * count).astype(jnp.float32).T
                places[p, k] = spread[:rows].astype(jnp.bfloat16)

    for p in range(outer):
        held = x_ref[p].reshape(group * count, packed)
        for k in range(inner):
            out = own_ref.at[p] if k == 0 else first_ref.at[p] if k == 1 else others_ref.at[k - 2, p]
            out[...] = jnp.dot(places[p, k], held, preferred_element_type=jnp.float32).astype(jnp.bfloat16)


def unpack_lines(arrived, sampled, me, inner, lines):
    outer, coils, count, packed = arrived.shape
    group = inner
    rows = group * lines
    tail = (coils * lines, packed)
    heads = [(outer,), (outer,), (2, outer)]
    return pl.pallas_call(
        unpack_kernel,
        out_shape=[jax.ShapeDtypeStruct((*h, *tail), jnp.bfloat16) for h in heads],
        grid_spec=pltpu.PrefetchScalarGridSpec(
            num_scalar_prefetch=1,
            grid=(coils // group,),
            in_specs=[
                pl.BlockSpec(sampled.shape, lambda i, me: (0, 0)),
                pl.BlockSpec((outer, group, count, packed), lambda i, me: (0, i, 0, 0)),
            ],
            out_specs=[
                pl.BlockSpec((*h, rows, packed), lambda i, me, h=h: (*(0 for _ in h), i, 0)) for h in heads
            ],
            scratch_shapes=[
                pltpu.VMEM((outer, inner, rows, group * count), jnp.bfloat16),
                pltpu.VMEM((sampled.shape[0], LANES), jnp.float32),
            ],
        ),
        compiler_params=pltpu.CompilerParams(vmem_limit_bytes=VMEM_BYTES),
        name="unpack_sampled",
    )(me, sampled, arrived)


def most_kernel(inner, outer, sampled_ref, o_ref):
    readouts, ky_count = sampled_ref.shape
    devices = inner * outer
    taken = sampled_ref[...].astype(jnp.float32).astype(jnp.bfloat16)
    line = lax.broadcasted_iota(jnp.int32, (ky_count, LANES), 0)
    lane = lax.broadcasted_iota(jnp.int32, (ky_count, LANES), 1)

    def sums(parts):
        return jnp.dot(
            taken, (line // (ky_count // parts) == lane).astype(jnp.bfloat16), preferred_element_type=jnp.float32
        )

    row = lax.broadcasted_iota(jnp.int32, (readouts, readouts), 0)
    readout = lax.broadcasted_iota(jnp.int32, (readouts, readouts), 1)
    together = (row // inner == readout // inner).astype(jnp.bfloat16)
    by_source = jnp.dot(together, sums(devices).astype(jnp.bfloat16), preferred_element_type=jnp.float32)
    o_ref[0, 0] = jnp.max(jnp.maximum(by_source, sums(outer))).astype(jnp.int32)


def first_kernel(inner, outer, me_ref, x_ref, *refs):
    params, (o_ref, packed_ref, most_ref, weight, tiles, picks) = refs[:5], refs[5:]
    window_kernel(0, me_ref, x_ref, *params, o_ref, weight, tiles)
    pack_kernel(True, me_ref, params[0], o_ref, packed_ref, picks)
    most_kernel(inner, outer, params[0], most_ref)


def first_chunk(lines_first, me, params, inner, outer, count):
    _, _, lines, readouts, kz_count = lines_first.shape
    rows, packed = inner * lines, 2 * kz_count
    shapes = [(readouts, rows, packed), (outer, inner, count, packed)]
    whole = [pl.BlockSpec(p.shape, lambda i, me: (0, 0)) for p in params]
    *arrays, most = pl.pallas_call(
        functools.partial(first_kernel, inner, outer),
        out_shape=[*(jax.ShapeDtypeStruct(s, jnp.bfloat16) for s in shapes), jax.ShapeDtypeStruct((1, 1), jnp.int32)],
        grid_spec=pltpu.PrefetchScalarGridSpec(
            num_scalar_prefetch=1,
            grid=(1,),
            in_specs=[pl.BlockSpec((2, inner, lines, readouts, kz_count), lambda i, me: (0, 0, 0, 0, 0)), *whole],
            out_specs=[
                *(pl.BlockSpec(s, lambda i, me, n=len(s): (0,) * n) for s in shapes),
                pl.BlockSpec(memory_space=pltpu.SMEM),
            ],
            scratch_shapes=[
                pltpu.VMEM((lines, readouts, kz_count), jnp.float32),
                pltpu.VMEM((packed // LANES, rows * readouts, LANES), jnp.float32),
                pltpu.VMEM((outer, inner, count, inner * rows), jnp.bfloat16),
            ],
        ),
        compiler_params=pltpu.CompilerParams(vmem_limit_bytes=VMEM_BYTES),
        name="window_and_pack",
    )(me, lines_first, *params)
    return *arrays, most[0, 0]


def pick_kernel(count, me_ref, slots_ref, table_ref, o_ref):
    o_ref[...] = jnp.zeros_like(o_ref)
    for p in range(slots_ref.shape[1]):
        pick = one_hot(slots_ref[me_ref[1], p], count)
        for part in range(2):
            o_ref[part, pl.ds(p * count, count), :] = jnp.dot(
                pick, table_ref[part, p], preferred_element_type=jnp.float32
            ).astype(jnp.bfloat16)


def pick_rows(table, slots, me, count, depth):
    outer = slots.shape[1]
    table = table.reshape(2, outer, table.shape[1] // outer, table.shape[2])
    shape = (2, depth, table.shape[3])
    return pl.pallas_call(
        functools.partial(pick_kernel, count),
        out_shape=jax.ShapeDtypeStruct(shape, jnp.bfloat16),
        grid_spec=pltpu.PrefetchScalarGridSpec(
            num_scalar_prefetch=1,
            grid=(1,),
            in_specs=[
                pl.BlockSpec(slots.shape, lambda i, me: (0, 0, 0, 0)),
                pl.BlockSpec(table.shape, lambda i, me: (0, 0, 0, 0)),
            ],
            out_specs=pl.BlockSpec(shape, lambda i, me: (0, 0, 0)),
        ),
        compiler_params=pltpu.CompilerParams(vmem_limit_bytes=VMEM_BYTES),
        name="pick_table_rows",
    )(me, slots, table)


def image_kernel(fresh, last, halves, lines, group, pieces, me_ref, *refs):
    xs, refs = refs[:pieces], list(refs[pieces:])
    x_ref, (maps_ref, kz_ref, ky_ref), refs = xs[0], refs[:3], refs[3:]
    acc_in = None if fresh else refs.pop(0)
    outs, (wide, by_line, hybrid, acc) = refs[:-4], refs[-4:]
    kz_count, ky_count = maps_ref.shape[-2:]
    depth = by_line.shape[1]
    width = ky_ref.shape[-1] // 2
    step = pl.program_id(0)

    @pl.when(step == 0)
    def _():
        acc[...] = jnp.zeros_like(acc) if fresh else acc_in[...]
        by_line[...] = jnp.zeros_like(by_line)

    if lines:
        stride = depth // (x_ref.shape[0] * pieces)

        def place(k, s, buffer):
            wide[buffer] = xs[k][s].astype(jnp.float32)
            source = s * pieces + (me_ref[3] ^ k) if pieces > 1 else s
            base = pl.multiple_of(source * stride, stride)
            for c in range(group):
                by_line[c, pl.ds(base, lines), :] = wide[buffer, pl.ds(lines * c, lines), :].astype(jnp.bfloat16)
            return 0

        if pieces > 1:
            for n in range(pieces * x_ref.shape[0]):
                place(n % pieces, n // pieces, n % BUFFERS)
        else:
            lax.fori_loop(0, x_ref.shape[0], lambda s, _: place(0, s, 0), 0)
    else:
        count = x_ref.shape[2]
        for c in range(group):
            for p in range(x_ref.shape[0]):
                by_line[c, p * count : (p + 1) * count, :] = x_ref[p, c]

    for c in range(group):
        mixed = lax.dot_general(
            kz_ref[...], by_line[c], (((1,), (1,)), ((), ())), preferred_element_type=jnp.float32
        )
        hybrid[c, :, :depth] = mixed[:kz_count].astype(jnp.bfloat16)
        hybrid[c, :, depth:] = mixed[kz_count:].astype(jnp.bfloat16)
    for c in range(group):
        image = jnp.dot(
            hybrid[c], ky_ref[...].reshape(2 * depth, 2 * width), preferred_element_type=jnp.float32
        )
        real, imag = image[:, :ky_count], image[:, width : width + ky_count]
        map_real = maps_ref[0, c, 0].astype(jnp.float32)
        map_imag = maps_ref[1, c, 0].astype(jnp.float32)
        acc[0] += map_real * real + map_imag * imag
        acc[1] += map_real * imag - map_imag * real

    @pl.when(step == pl.num_programs(0) - 1)
    def _():
        if last and halves == 2:
            keep_ref, send_ref = outs
            rows = ky_count // 2
            lower = me_ref[0] == 0
            for part in range(2):
                low, high = acc[part, :, :rows], acc[part, :, rows:]
                keep_ref[part] = jnp.where(lower, low, high)
                send_ref[part] = jnp.where(lower, high, low).astype(send_ref.dtype)
        else:
            outs[0][...] = acc[...]


def image_chunk(arrived, maps, kz, ky, acc, me, group, lines, start, coils, last, halves):
    kz_count, ky_count = maps.shape[-2:]
    packed = arrived[0].shape[-1]
    depth = ky.shape[1]
    if lines:
        x_specs = block_specs(arrived, group * lines)
    else:
        group = 2 if last else group
        x_specs = [
            pl.BlockSpec((x.shape[0], group, *x.shape[2:]), lambda i, me: (0, i, 0, 0)) for x in arrived
        ]
    wide = (BUFFERS, max(group * lines, 8), packed)
    in_specs = [
        *x_specs,
        pl.BlockSpec((2, group, 1, kz_count, ky_count), lambda i, me: (0, i + start // group, 0, 0, 0)),
        pl.BlockSpec(kz.shape, lambda i, me: (0, 0)),
        pl.BlockSpec(ky.shape, lambda i, me: (0, 0, 0)),
    ]
    operands = [*arrived, maps, kz, ky]
    if acc is not None:
        in_specs.append(pl.BlockSpec(acc.shape, lambda i, me: (0, 0, 0)))
        operands.append(acc)
    image_shape = (2, kz_count, ky_count)
    outs = [jax.ShapeDtypeStruct(image_shape, jnp.float32)]
    if last and halves == 2:
        half_shape = (2, kz_count, ky_count // 2)
        outs = [jax.ShapeDtypeStruct(half_shape, jnp.float32), jax.ShapeDtypeStruct(half_shape, jnp.bfloat16)]
    return pl.pallas_call(
        functools.partial(image_kernel, acc is None, last, halves, lines, group, len(arrived)),
        out_shape=outs,
        grid_spec=pltpu.PrefetchScalarGridSpec(
            num_scalar_prefetch=1,
            grid=(coils // group,),
            in_specs=in_specs,
            out_specs=[pl.BlockSpec(o.shape, lambda i, me: (0, 0, 0)) for o in outs],
            scratch_shapes=[
                pltpu.VMEM(wide, jnp.float32),
                pltpu.VMEM((group, depth, packed), jnp.bfloat16),
                pltpu.VMEM((group, kz_count, 2 * depth), jnp.bfloat16),
                pltpu.VMEM(image_shape, jnp.float32),
            ],
        ),
        compiler_params=pltpu.CompilerParams(vmem_limit_bytes=VMEM_BYTES),
        name="image_of_coils",
    )(me, *operands)


def ranks(taken):
    lines = taken.shape[-1]
    before = jnp.asarray(np.triu(np.ones((lines, lines), np.float32), 1).astype(ml_dtypes.bfloat16))
    flat = taken.reshape(-1, lines).astype(jnp.bfloat16)
    rank = jnp.dot(flat, before, preferred_element_type=jnp.float32)
    return jnp.where(flat > 0, rank, -1.0).reshape(taken.shape)


def on_device(kspace, sensitivity, sampled, pole_y, order_y, pole_z, order_z):
    _, coils, readouts, lines, kz_count = kspace.shape
    devices = lax.axis_size("ro")
    halves = lax.axis_size("coil")
    ky_count = lines * devices
    stride = round_up(lines, 16)
    inner = 16 // math.gcd(lines, 16)
    outer = devices // inner
    parts = [(coils,), ()] if inner != 4 or coils != sum(FIRST + LATER) else [FIRST, LATER]
    planned = len(parts[1]) > 0 and FIRST[0] == STRAIGHT[0] == inner
    place = lax.axis_index("ro")
    me = jnp.stack([lax.axis_index("coil"), place, place // inner, place % inner]).astype(jnp.int32)
    lines_first = jnp.swapaxes(kspace, 2, 3)
    maps = jnp.swapaxes(sensitivity, 3, 4)
    params = (sampled, pole_y, order_y, pole_z, order_z)
    kz = kz_table(kz_count)
    tables = ky_tables(ky_count, round_up(ky_count, LANES))
    ky = jnp.pad(tables.reshape(2, devices, lines, -1), ((0, 0), (0, 0), (0, stride - lines), (0, 0))).reshape(
        2, devices * stride, -1
    )

    def window(planes, start, count):
        return window_chunk(lines_first, me, params, inner, planes, start, count)

    def image(arrived, rows, by_line, start, count, acc, last=False):
        return image_chunk(
            arrived, maps, kz, rows, acc, me, inner, lines if by_line else 0, start, count, last, halves
        )

    def to_place(array, k):
        return lax.ppermute(array, "ro", [(a, a ^ k) for a in range(devices)])

    def in_plane(own, first, others):
        across = to_place(others, 2)
        return [own, to_place(first, 1), across, to_place(across[1], 1)]

    def to_planes(packed):
        same_place = [[p * inner + i for p in range(outer)] for i in range(inner)]
        return lax.all_to_all(
            packed, "ro", split_axis=0, concat_axis=0, tiled=True, axis_index_groups=same_place
        )

    def finish(result):
        if halves == 2:
            keep, give = result
            whole = keep + lax.ppermute(give, "coil", [(0, 1), (1, 0)]).astype(jnp.float32)
        else:
            whole = lax.psum_scatter(result[0], "coil", scatter_dimension=2, tiled=True)
        return jnp.swapaxes(whole, 1, 2)[:, None]

    def straight(first, plan):
        starts = [sum(plan[:i]) for i in range(len(plan))]
        acc, arrived = None, []
        for i, start in enumerate(starts):
            sent = first if i == 0 else window(0, start, plan[i])[0]
            if i >= 2:
                acc = image([arrived[i - 2]], ky, True, starts[i - 2], plan[i - 2], acc)[0]
                sent, acc = lax.optimization_barrier((sent, acc))
            arrived.append(lax.all_to_all(sent, "ro", split_axis=0, concat_axis=0, tiled=True))
        for i in range(max(len(plan) - 2, 0), len(plan)):
            result = image([arrived[i]], ky, True, starts[i], plan[i], acc, i == len(plan) - 1)
            acc = result[0]
        return finish(result)

    if not planned:
        return straight(window(0, 0, coils)[0], (coils,))

    starts = [sum((FIRST + LATER)[:i]) for i in range(len(FIRST + LATER))]
    first_starts, later_starts = starts[: len(FIRST)], starts[len(FIRST) :]

    def pack(held, slots):
        return pack_lines(held, slots, me, outer, inner, lines, SLOTS)

    def spread(part):
        return in_plane(*unpack_lines(part, sampled, me, inner, lines))

    def by_planes(one):
        plane_slots = ranks(sampled.reshape(readouts, outer, inner * lines))
        for_plane = plane_slots.reshape(readouts, devices, 1, lines)
        rows = pick_rows(tables, plane_slots[:, :, None], me, SLOTS, round_up(outer * SLOTS, LANES))
        second = window(0, first_starts[1], FIRST[1])
        third = window(outer, later_starts[0], LATER[0])
        one = to_planes(one)
        two, one, third = lax.optimization_barrier((pack(second, sampled), one, third))
        two = to_planes(two)
        third = in_plane(*third)
        one = spread(one)
        here, one, rows = lax.optimization_barrier((for_plane, one, rows))
        three, two = lax.optimization_barrier((pack(third, here), two))
        three = to_planes(three)
        acc = image(one, ky, True, first_starts[0], FIRST[0], None)[0]
        after, acc = lax.optimization_barrier((me, acc))
        two = spread(two)
        fourth = in_plane(*window_chunk(lines_first, after, params, inner, outer, later_starts[1], LATER[1]))
        four, acc, two, three = lax.optimization_barrier((pack(fourth, for_plane), acc, two, three))
        four = to_planes(four)
        acc = image(two, ky, True, first_starts[1], FIRST[1], acc)[0]
        acc = image([three], rows, False, later_starts[0], LATER[0], acc)[0]
        return finish(image([four], rows, False, later_starts[1], LATER[1], acc, True))

    first, packed, most = first_chunk(lines_first, me, params, inner, outer, SLOTS)
    return lax.cond(
        most <= SLOTS,
        lambda first, packed: by_planes(packed),
        lambda first, packed: straight(first, STRAIGHT),
        first,
        packed,
    )


def solution(mesh):
    return jax.shard_map(
        on_device,
        mesh=mesh,
        in_specs=(
            P(None, "coil", None, "ro", None),
            P(None, "coil", "ro", None, None),
            P(),
            P(),
            P(),
            P(),
            P(),
        ),
        out_specs=P(None, "ro", "coil", None),
        check_vma=False,
    )
```
